32 devices in a mesh: pipe: 2 (over x), dp: 16 (over z, y, core).
Axes of the slice: x: 2, y: 2, z: 4, core: 2. Of those that a mesh axis runs over, the one named last changes fastest.
Arguments:
- visual_fragments: bfloat16 [2, 16, 64, 1152], P(None, 'dp'), may hold values from -6 to 6
- widening_kernel: bfloat16 [2, 1152, 2176], P('pipe', None, 'dp'), may hold values from -0.1875 to 0.1875
- narrowing_kernel: bfloat16 [2, 2176, 1152], P('pipe', 'dp'), may hold values from -0.125 to 0.125
- caption_outputs: bfloat16 [288, 1152], P(('pipe', 'dp')), may hold values from -6 to 6
- earlier_averaged: float32 [256, 1152], P(('pipe', 'dp')), may hold values from -6 to 6
- match_targets: int32 [288], replicated, may hold values from 0 to 287, each once
- score_scaling: float32 [1], replicated, may hold values from 5 to 15
- score_shift: float32 [1], replicated, may hold values from -4 to -2
Outputs:
- image_grad: float32 [288, 1152], P(('pipe', 'dp'))
- text_grad: float32 [288, 1152], P(('pipe', 'dp'))
The draws below stay inside these ranges and needn't reach their ends.
Inputs may be any that keep to these rules, and one draw needn't show every extreme that they name: match_targets is a permutation: every text is the positive of exactly one image.
All inputs are finite; a program needn't handle non-finite values.
Results may differ from the reference program's by a relative error of at most 0.017.
Values may be sent and summed in bfloat16 or wider, within the bound.
A program may use at most 128 MiB of HBM per device.

```python
import math
import jax
import jax.numpy as jnp
from jax import lax

E = 1152
FFW = 2176
PATCH = 64
IMG_MB = 1
PRIOR_DEV = 8
LAYERS = 2
MICRO = 2
IMG_MICRO = 16
TOWER_IMAGES = 32
PRIOR = 256
IMAGES = 288
TEXTS = 288
N_PIPE = 2
N_DP = 16


def shard_levels(stream_key, dims, cuts, least, high):
    loudness, own = 1.0, jax.random.fold_in(stream_key, 6)
    for position, shards_of in cuts:
        draws = jnp.exp(jax.random.uniform(jax.random.fold_in(own, position), (shards_of,), jnp.float32, least / len(cuts), high / len(cuts)))
        loudness = loudness * jnp.repeat(draws, dims[position] // shards_of).reshape([-1 if axis == position else 1 for axis in range(len(dims))])
    return loudness


def centred(rng, shape, scale, reach, split=(), kind=jnp.bfloat16):
    entries = jax.random.normal(rng, shape, jnp.float32) * scale
    if len(split) > 0:
        entries = shard_levels(rng, shape, split, -0.22, 0.18) * entries
    return jnp.clip(entries, min=-reach, max=reach).astype(kind)


def setup_inputs(seed: int = 0) -> dict:
    key_of = jax.random.split(jax.random.key(seed), 9)
    visual_fragments = centred(key_of[0], (MICRO, IMG_MICRO, PATCH, E), 1.0, 6.0, ((1, 16),))
    widening_kernel = centred(key_of[1], (LAYERS, E, FFW), E ** -0.5, 0.1875, ((0, 2), (2, 16)))
    narrowing_kernel = centred(key_of[2], (LAYERS, FFW, E), FFW ** -0.5, 0.125, ((0, 2), (1, 16)))
    caption_outputs = centred(key_of[3], (TEXTS, E), 1.0, 6.0, ((0, 32),))
    earlier_averaged = centred(key_of[4], (PRIOR, E), 1.0, 6.0, ((0, 32),), jnp.float32)
    match_targets = jax.random.permutation(key_of[5], IMAGES).astype(jnp.int32)
    score_scaling = jnp.clip(jnp.exp(jax.random.uniform(key_of[6], (1,), jnp.float32, math.log(5.0), math.log(15.0))), 5.0, 15.0)
    score_shift = jnp.clip(jax.random.uniform(key_of[7], (1,), jnp.float32, -4.0, -2.0), -4.0, -2.0)
    return dict(visual_fragments=visual_fragments, widening_kernel=widening_kernel, narrowing_kernel=narrowing_kernel, caption_outputs=caption_outputs, earlier_averaged=earlier_averaged, match_targets=match_targets, score_scaling=score_scaling, score_shift=score_shift)


def layer_norm(hidden_rows):
    values = hidden_rows.astype(jnp.float32)
    centre = lax.optimization_barrier(jnp.mean(values, axis=-1, keepdims=True))
    shifted = values - centre
    variance = lax.optimization_barrier(jnp.mean(shifted * shifted, axis=-1, keepdims=True))
    return (shifted * lax.rsqrt(variance + 1e-06)).astype(jnp.bfloat16)

def section_block(hidden_rows, w_up, w_down):
    normed = layer_norm(hidden_rows)
    pre_act = jnp.dot(normed, w_up, preferred_element_type=jnp.float32)
    activated = jax.nn.gelu(pre_act, approximate=True).astype(jnp.bfloat16)
    updated = hidden_rows.astype(jnp.float32) + jnp.dot(activated, w_down, preferred_element_type=jnp.float32)
    return updated.astype(jnp.bfloat16)

def unit_rows(values):
    values = values.astype(jnp.float32)
    total = lax.optimization_barrier(jnp.sum(values * values, axis=-1, keepdims=True))
    return (values * lax.rsqrt(total + 1e-06)).astype(jnp.bfloat16)

def coupling_factors(picture_group, source_caption_tile, match_entries, target_tile, sharpness_factor, shift_addend):
    similarity_scores = sharpness_factor * jnp.dot(picture_group, source_caption_tile.T, preferred_element_type=jnp.float32) + shift_addend
    matching_couples = match_entries[:, None] == target_tile[None, :]
    coefficient_grid = jnp.where(matching_couples, -sharpness_factor * jax.nn.sigmoid(-similarity_scores), sharpness_factor * jax.nn.sigmoid(similarity_scores))
    return coefficient_grid.astype(jnp.bfloat16)

def reference(visual_fragments, widening_kernel, narrowing_kernel, caption_outputs, earlier_averaged, match_targets, score_scaling, score_shift):

    def one_micro(micro_tokens):
        tokens = micro_tokens.reshape(IMG_MICRO * PATCH, E)
        for layer in range(LAYERS):
            tokens = section_block(tokens, widening_kernel[layer], narrowing_kernel[layer])
        return lax.optimization_barrier(jnp.mean(tokens.astype(jnp.float32).reshape(IMG_MICRO, PATCH, E), axis=1))
    pooled = lax.map(one_micro, visual_fragments).reshape(TOWER_IMAGES, E)
    tower_emb = unit_rows(pooled).reshape(N_PIPE * N_DP, IMG_MB, E)
    prior_emb = unit_rows(earlier_averaged).reshape(N_PIPE * N_DP, PRIOR_DEV, E)
    picture_vectors = jnp.concatenate([tower_emb, prior_emb], axis=1).reshape(IMAGES, E)
    caption_vectors = unit_rows(caption_outputs)
    target_tile = jnp.arange(TEXTS, dtype=jnp.int32)
    coefficient_grid = coupling_factors(picture_vectors, caption_vectors, match_targets, target_tile, score_scaling[0], score_shift[0])
    image_grad = jnp.dot(coefficient_grid, caption_vectors, preferred_element_type=jnp.float32)
    text_grad = jnp.dot(coefficient_grid.T, picture_vectors, preferred_element_type=jnp.float32)
    return (image_grad, text_grad)
```

```python
import functools

import jax
import jax.numpy as jnp
from jax import lax
from jax.experimental import pallas as pl
from jax.experimental.pallas import tpu as pltpu
from jax.sharding import PartitionSpec as P

F32, BF16 = jnp.float32, jnp.bfloat16
SLOT = 32
MID = 16
TILE = 256
NT = (((1,), (1,)), ((), ()))
NN = (((1,), (0,)), ((), ()))


def dot(a, b, dims):
    return lax.dot_general(a, b, dims, preferred_element_type=F32)


def layer_norm(values):
    shifted = values - jnp.mean(values, axis=-1, keepdims=True)
    variance = jnp.mean(shifted * shifted, axis=-1, keepdims=True)
    return (shifted * lax.rsqrt(variance + 1e-06)).astype(BF16)


def unit_rows(values):
    total = jnp.sum(values * values, axis=-1, keepdims=True)
    return (values * lax.rsqrt(total + 1e-06)).astype(BF16)


def kernel(
    cfg,
    scale_ref, shift_ref, ids_ref, tids_ref, x_ref, w_ref, cap_ref, prior_ref,
    img_ref, txt_ref, *rest,
):
    n_pipe, n_dp, micros, rows, width, ff, texts, priors, spill = cfg
    if spill:
        eg, *rest = rest
    else:
        *rest, eg = rest
    (own, chunk, ug, dg, xg, part, sc, rc, sz, rz, ma, ma2, mx, mx2, tp, tall,
     w_s, w_r, x_s, x_r, c_s, c_r, z_s, z_r, h_s, h_r, tp_s, tp_r, ta_s, ta_r,
     ez_s, ez_r, ey_s, ey_r, ex_s, ex_r, ec_s, ec_r, loc) = rest
    p, d = lax.axis_index("pipe"), lax.axis_index("dp")
    c, y, z = d % 2, (d // 2) % 2, d // 4
    zb, zp = z % 2, z // 2
    nz = n_dp // 4
    nzp = nz // 2
    groups = 2 * nzp
    last = n_pipe - 1
    oc, oz = 1 - c, 1 - zb

    def at(z_, y_, c_):
        return (z_ * 2 + y_) * 2 + c_

    d_c, d_y, d_z = at(z, y, oc), at(z, 1 - y, c), at(zp * 2 + oz, y, c)

    def copy(src, dst, s, r, pipe, dp):
        return pltpu.make_async_remote_copy(
            src_ref=src, dst_ref=dst, send_sem=s, recv_sem=r,
            device_id=(pipe, dp), device_id_type=pl.DeviceIdType.MESH)

    def arrived(dst, r):
        copy(dst, dst, loc.at[0], r, p, d_c).wait_recv()

    def left(src, s):
        copy(src, src, s, loc.at[0], p, d_c).wait_send()

    barrier = pltpu.get_barrier_semaphore()
    total = n_pipe * n_dp

    def greet(i, _):
        t = (p * n_dp + d + i) % total
        pl.semaphore_signal(barrier, inc=1, device_id=(t // n_dp, t % n_dp),
                            device_id_type=pl.DeviceIdType.MESH)
        return 0

    lax.fori_loop(1, total, greet, 0)

    own[...] = jnp.zeros_like(own)
    own[0:texts, :] = unit_rows(cap_ref[...].astype(F32))
    own[MID:MID + priors, :] = unit_rows(prior_ref[...])

    @pl.when(p == 0)
    def _():
        for m in range(micros):
            xg[zb, m, c] = x_ref[m]

    q = zp * 2 + y

    def wslot(ref, q_):
        return ref.at[pl.ds(pl.multiple_of(q_ * ff, 16), ff), :]

    for k, ref in enumerate((ug, dg)):
        ref[pl.ds(pl.multiple_of(q * ff, 16), ff), :] = w_ref[k]
    pl.semaphore_wait(barrier, total - 1)

    big = ((0, ug), (1, dg))

    def w_own_y(k, ref):
        return copy(w_ref.at[k], wslot(ref, q), w_s.at[k, 0], w_r.at[k, q], p, d_y)

    def w_own_z(k, ref, i):
        t = at(((zp + i) % nzp) * 2 + zb, y, c)
        return copy(w_ref.at[k], wslot(ref, q), w_s.at[k, i], w_r.at[k, q], p, t)

    def w_fwd(k, ref, i):
        q_ = ((zp + i) % nzp) * 2 + y
        return copy(wslot(ref, q_), wslot(ref, q_), w_s.at[k, nzp + i], w_r.at[k, q_], p, d_y)

    def x_c(m):
        return copy(xg.at[zb, m, c], xg.at[zb, m, c], x_s.at[0, m], x_r.at[zb, m, c], p, d_c)

    def x_z(m):
        return copy(xg.at[zb, m, c], xg.at[zb, m, c], x_s.at[1, m], x_r.at[zb, m, c], p, d_z)

    def x_f(m):
        return copy(xg.at[oz, m, c], xg.at[oz, m, c], x_s.at[2, m], x_r.at[oz, m, c], p, d_c)

    for k, ref in big:
        for i in range(1, nzp):
            w_own_z(k, ref, i).start()
        w_own_y(k, ref).start()
        if k == 0:
            @pl.when(p == 0)
            def _():
                for m in range(micros):
                    x_c(m).start()
                    x_z(m).start()

    def eslot(index, count):
        return eg.at[pl.ds(index, count)]

    e_own = ((c * n_pipe + p) * 2 + y) * nz + z
    e_y, e_x, e_c = ((c * n_pipe + p) * 2 + y) * nz, (c * n_pipe + p) * 2 * nz, c * n_pipe * 2 * nz

    def e_z(i):
        t = (z + i) % nz
        return copy(own, eg.at[e_own], ez_s.at[i], ez_r.at[z], p, at(t, y, c))

    for i in range(1, nz):
        e_z(i).start()
    keep = pltpu.make_async_copy(own, eg.at[e_own], loc.at[1])
    keep.start()

    for k, ref in big:
        for i in range(1, nzp):
            q_ = ((zp + i) % nzp) * 2 + y
            arrived(wslot(ref, q_), w_r.at[k, q_])
            w_fwd(k, ref, i).start()

    keep.wait()
    for i in range(1, nz):
        t = (z + i) % nz
        arrived(eg.at[e_y + t], ez_r.at[t])
    send_y = copy(eslot(e_y, nz), eslot(e_y, nz), ey_s, ey_r, p, d_y)
    send_y.start()

    def tokens_on():
        for m in range(micros):
            arrived(xg.at[oz, m, c], x_r.at[oz, m, c])
            x_f(m).start()

    def tokens_here():
        for m in range(micros):
            arrived(xg.at[zb, m, oc], x_r.at[zb, m, oc])
            arrived(xg.at[oz, m, oc], x_r.at[oz, m, oc])

    @pl.when(p == 0)
    def _():
        tokens_on()

    e_yo = ((c * n_pipe + p) * 2 + 1 - y) * nz
    arrived(eslot(e_yo, nz), ey_r)

    def e_xs(i):
        return copy(eslot(e_x, 2 * nz), eslot(e_x, 2 * nz), ex_s.at[i], ex_r.at[p],
                    (p + i) % n_pipe, d)

    for i in range(1, n_pipe):
        e_xs(i).start()

    for k, ref in big:
        for i in range(nzp):
            q_ = ((zp + i) % nzp) * 2 + 1 - y
            arrived(wslot(ref, q_), w_r.at[k, q_])

    def emb_finish():
        for i in range(1, n_pipe):
            t = (p + i) % n_pipe
            arrived(eslot((c * n_pipe + t) * 2 * nz, 2 * nz), ex_r.at[t])
        send_c = copy(eslot(e_c, n_pipe * 2 * nz), eslot(e_c, n_pipe * 2 * nz), ec_s, ec_r, p, d_c)
        send_c.start()
        arrived(eslot(oc * n_pipe * 2 * nz, n_pipe * 2 * nz), ec_r)
        send_c.wait_send()

    span = micros * 2 * rows
    tile = min(TILE, span)
    tiles = span // tile
    per = tile // rows
    mt = per // 2

    def activate(b, j):
        values = xg[b, pl.ds(j * mt, mt)].reshape(tile, width).astype(F32)
        act = jax.nn.gelu(dot(layer_norm(values), ug[...], NT), approximate=True)
        return values, act.astype(BF16)

    def hidden_out(m):
        return copy(sz.at[1, m], xg.at[zb, m, c], h_s.at[m], h_r.at[m],
                    jnp.minimum(p + 1, last), d)

    def to_core(b, m):
        return copy(sc.at[b, m], rc.at[b, m], c_s.at[b, m], c_r.at[b, m], p, d_c)

    def to_z(m):
        return copy(sz.at[0, m], rz.at[m], z_s.at[m], z_r.at[m], p, d_z)

    @pl.when(p > 0)
    def _():
        emb_finish()
        for m in range(micros):
            arrived(xg.at[zb, m, c], h_r.at[m])
            x_c(m).start()
            x_z(m).start()
        tokens_on()

    tokens_here()

    @pl.when(p < last)
    def _():
        for b in (oz, zb):
            def step(j, _, b=b):
                _, act = activate(b, j)
                out = dot(act, dg[...], NN)
                part[b, pl.ds(j * mt, mt)] = out.reshape(mt, 2, rows, width)
                return 0

            lax.fori_loop(0, tiles, step, 0)
            for m in range(micros):
                sc[b, m] = part[b, m, oc].astype(BF16)
                to_core(b, m).start()
            if b is oz:
                for m in range(micros):
                    arrived(rc.at[oz, m], c_r.at[oz, m])
                    sz[0, m] = (part[oz, m, c] + rc[oz, m].astype(F32)).astype(BF16)
                    to_z(m).start()
        for m in range(micros):
            arrived(rc.at[zb, m], c_r.at[zb, m])
            arrived(rz.at[m], z_r.at[m])
            new = part[zb, m, c] + rc[zb, m].astype(F32) + rz[m].astype(F32)
            sz[1, m] = (new + xg[zb, m, c].astype(F32)).astype(BF16)
            hidden_out(m).start()
        for m in range(micros):
            for b in range(2):
                left(sc.at[b, m], c_s.at[b, m])
            left(sz.at[0, m], z_s.at[m])
            left(sz.at[1, m], h_s.at[m])

    @pl.when(p == 0)
    def _():
        emb_finish()

    scale, shift = scale_ref[0], shift_ref[0]
    n_rows = total * SLOT
    cs = chunk.shape[0] if spill else n_rows
    ids_w = ids_ref.shape[1]

    def column(ref, first, count, limit):
        lane = lax.broadcasted_iota(jnp.int32, (count, limit), 1)
        row = lax.broadcasted_iota(jnp.int32, (count, limit), 0)
        return jnp.max(jnp.where(lane == row + first, ref[...], -1), axis=1, keepdims=True)

    def weigh(scores, row_ids, col_ids, keep_mask):
        logits = scale * scores + shift
        positive = row_ids == col_ids
        w = jnp.where(positive, -scale * jax.nn.sigmoid(-logits), scale * jax.nn.sigmoid(logits))
        return jnp.where(keep_mask, w, 0.0).astype(BF16)

    def block(j):
        if not spill:
            return eg[...].reshape(n_rows, width), ids_ref[...]
        fetch = pltpu.make_async_copy(eg.at[pl.ds(j * (cs // SLOT), cs // SLOT)], chunk2, loc.at[1])
        fetch.start()
        fetch.wait()
        return chunk2[...].reshape(cs, width), ids_ref[:, pl.ds(pl.multiple_of(j * cs, cs), cs)]

    chunk2 = chunk.reshape(cs // SLOT, SLOT, width) if spill else None
    own_v = own[...]
    own_ids = column(ids_ref, e_own * SLOT, SLOT, ids_w)
    kind_r = lax.broadcasted_iota(jnp.int32, (SLOT, cs), 0)
    kind_c = lax.broadcasted_iota(jnp.int32, (SLOT, cs), 1) % SLOT
    text_c = kind_c < texts
    prior_c = (kind_c >= MID) & (kind_c < MID + priors)
    mask = ((kind_r < texts) & prior_c) | ((kind_r >= MID) & text_c)

    def early(j, acc):
        e, ids = block(j)
        w = weigh(dot(own_v, e, NT), own_ids, ids, mask)
        return acc + dot(w, e, NN)

    if spill:
        grads = lax.fori_loop(0, n_rows // cs, early, jnp.zeros((SLOT, width), F32))
    else:
        grads = early(0, 0.0)
    img_ref[1:1 + priors, :] = grads[MID:MID + priors]

    @pl.when(p == last)
    def _():
        def step(i, _):
            b, j = i // tiles, i % tiles
            values, act = activate(b, j)
            ma[i] = jnp.mean(act.astype(F32).reshape(per, rows, -1), axis=1)
            mx[i] = jnp.mean(values.reshape(per, rows, width), axis=1)
            return 0

        lax.fori_loop(0, 2 * tiles, step, 0)
        for i in range(2 * tiles):
            ma2[i * per:(i + 1) * per, :] = ma[i]
            mx2[i * per:(i + 1) * per, :] = mx[i]
        t = zb * 2 + c
        tp[t] = dot(ma2[...].astype(BF16), dg[...], NN)

        def t_out(i):
            t_ = (t + i) % 4
            return copy(tp.at[t], tp.at[t], tp_s.at[i], tp_r.at[t], p,
                        at(zp * 2 + t_ // 2, y, t_ % 2))

        for i in range(1, 4):
            t_out(i).start()
        for i in range(1, 4):
            t_ = (t + i) % 4
            arrived(tp.at[t_], tp_r.at[t_])
        pooled = mx2[...] + (tp[0] + tp[1]) + (tp[2] + tp[3])
        tall[q] = unit_rows(pooled).astype(F32)

        def spread(i, _):
            s = (last * groups + q + i) % (n_pipe * groups)
            g = s % groups
            copy(tall.at[q], tall.at[q], ta_s.at[i], ta_r.at[q], s // groups,
                 at((g // 2) * 2 + zb, g % 2, c)).start()
            return 0

        lax.fori_loop(1, n_pipe * groups, spread, 0)
        for i in range(1, 4):
            left(tp.at[t], tp_s.at[i])
        for i in range(1, groups):
            g = (q + i) % groups
            arrived(tall.at[g], ta_r.at[g])
        for i in range(1, n_pipe * groups):
            left(tall.at[q], ta_s.at[i])

    @pl.when(p != last)
    def _():
        for g in range(groups):
            arrived(tall.at[g], ta_r.at[g])

    n_t = tall.shape[0] * tall.shape[1]
    towers = tall[...].reshape(n_t, width).astype(BF16)
    t_ids = tids_ref[...][:, :n_t]
    rmask = lax.broadcasted_iota(jnp.int32, (SLOT, n_t), 0) < texts
    w = weigh(dot(own_v, towers, NT), own_ids, t_ids, rmask)
    txt_ref[...] = (grads + dot(w, towers, NN))[:texts]

    mine = (zb * micros + p) * 2 + c
    pick = lax.broadcasted_iota(jnp.int32, (tall.shape[1], width), 0) == mine
    row = jnp.sum(jnp.where(pick, tall[q], 0.0), axis=0, keepdims=True)
    row8 = jnp.broadcast_to(row, (8, width)).astype(BF16)
    row_id = column(tids_ref, q * tall.shape[1] + mine, 1, tids_ref.shape[1])
    row_ids = jnp.broadcast_to(row_id, (8, 1))

    def late(j, acc):
        e, ids = block(j)
        w = weigh(dot(row8, e, NT), row_ids, ids, text_c[:8])
        return acc + dot(w, e, NN)

    if spill:
        g_row = lax.fori_loop(0, n_rows // cs, late, jnp.zeros((8, width), F32))
    else:
        g_row = late(0, 0.0)
    img_ref[0:1, :] = g_row[0:1]

    for k, ref in big:
        for i in range(nzp):
            left(w_ref.at[k], w_s.at[k, i])
        for i in range(1, nzp):
            left(w_ref.at[k], w_s.at[k, nzp + i])
    for m in range(micros):
        for i in range(3):
            left(xg.at[zb, m, c], x_s.at[i, m])
    for i in range(1, nz):
        left(own, ez_s.at[i])
    send_y.wait_send()
    for i in range(1, n_pipe):
        left(eslot(e_x, 2 * nz), ex_s.at[i])


def body(vis, up, down, cap, prior, match, scale, shift):
    n_pipe, n_dp = lax.axis_size("pipe"), lax.axis_size("dp")
    micros, img_mb, patch, width = vis.shape
    rows = img_mb * patch
    shard = up.shape[2]
    ff = -(-shard // 16) * 16
    texts, priors = cap.shape[0], prior.shape[0]
    nz, total = n_dp // 4, n_pipe * n_dp
    nzp = nz // 2
    groups = 2 * nzp
    w = jnp.stack([up[0].T, down[0]])
    w = jnp.pad(w, ((0, 0), (0, ff - shard), (0, 0)))
    per = texts
    table = match.reshape(n_pipe, nz, 2, 2, per).transpose(3, 0, 2, 1, 4).reshape(total, per)
    own_text = jnp.arange(total * texts, dtype=jnp.int32).reshape(n_pipe, nz, 2, 2, texts)
    own_text = own_text.transpose(3, 0, 2, 1, 4).reshape(total, texts)
    ids = jnp.concatenate([
        jnp.pad(own_text, ((0, 0), (0, MID - texts)), constant_values=-2),
        jnp.pad(table[:, 1:], ((0, 0), (0, SLOT - MID - priors)), constant_values=-2),
    ], axis=1).reshape(1, total * SLOT)
    tids = match.reshape(micros, nzp, 2, 2, 2, per)[..., 0].transpose(1, 3, 2, 0, 4).reshape(1, -1)
    n_t = tids.shape[1]
    tids = jnp.pad(tids, ((0, 0), (0, -n_t % 128)), constant_values=-2)
    spill = total > 64
    cfg = (n_pipe, n_dp, micros, rows, width, ff, texts, priors, spill)
    span = micros * 2 * rows
    tile = min(TILE, span)
    tiles, kept = span // tile, tile // rows
    imgs = 4 * micros
    ffg = groups * ff
    vm = pl.BlockSpec(memory_space=pltpu.VMEM)
    sm = pl.BlockSpec(memory_space=pltpu.SMEM)
    dma = pltpu.SemaphoreType.DMA
    outs = [jax.ShapeDtypeStruct((texts, width), F32)] * 2
    out_specs = [vm, vm]
    eg_shape = (total, SLOT, width)
    scratch = [
        pltpu.VMEM((SLOT, width), BF16),
        pltpu.VMEM((1024, width) if spill else (16, width), BF16),
        pltpu.VMEM((ffg, width), BF16),
        pltpu.VMEM((ffg, width), BF16),
        pltpu.VMEM((2, micros, 2, rows, width), BF16),
        pltpu.VMEM((2, micros, 2, rows, width), F32),
        pltpu.VMEM((2, micros, rows, width), BF16),
        pltpu.VMEM((2, micros, rows, width), BF16),
        pltpu.VMEM((2, micros, rows, width), BF16),
        pltpu.VMEM((micros, rows, width), BF16),
        pltpu.VMEM((2 * tiles, kept, ffg), F32),
        pltpu.VMEM((imgs, ffg), F32),
        pltpu.VMEM((2 * tiles, kept, width), F32),
        pltpu.VMEM((imgs, width), F32),
        pltpu.VMEM((4, imgs, width), F32),
        pltpu.VMEM((groups, imgs, width), F32),
        dma((2, 2 * nzp)), dma((2, groups)),
        dma((3, micros)), dma((2, micros, 2)),
        dma((2, micros)), dma((2, micros)),
        dma((micros,)), dma((micros,)),
        dma((micros,)), dma((micros,)),
        dma((4,)), dma((4,)),
        dma((n_pipe * groups,)), dma((groups,)),
        dma((nz,)), dma((nz,)),
        dma, dma,
        dma((n_pipe,)), dma((n_pipe,)),
        dma, dma,
        dma((2,)),
    ]
    if spill:
        outs = outs + [jax.ShapeDtypeStruct(eg_shape, BF16)]
        out_specs = out_specs + [pl.BlockSpec(memory_space=pl.ANY)]
    else:
        scratch = scratch + [pltpu.VMEM(eg_shape, BF16)]
    result = pl.pallas_call(
        functools.partial(kernel, cfg),
        out_shape=outs,
        in_specs=[sm, sm, vm, vm, vm, vm, vm, vm],
        out_specs=out_specs,
        scratch_shapes=scratch,
        compiler_params=pltpu.CompilerParams(
            collective_id=0, has_side_effects=True, vmem_limit_bytes=60 * 2**20),
    )(scale, shift, ids, tids, vis.reshape(micros, rows, width), w, cap, prior)
    return result[0], result[1]


def solution(mesh):
    placed = (
        P(None, "dp", None, None),
        P("pipe", None, "dp"),
        P("pipe", "dp", None),
        P(("pipe", "dp"), None),
        P(("pipe", "dp"), None),
        P(),
        P(),
        P(),
    )
    return jax.shard_map(
        body,
        mesh=mesh,
        in_specs=placed,
        out_specs=(P(("pipe", "dp"), None), P(("pipe", "dp"), None)),
        check_vma=False,
    )
```

```python
import functools

import jax
import jax.numpy as jnp
from jax import lax
from jax.experimental import pallas as pl
from jax.experimental.pallas import tpu as pltpu
from jax.sharding import PartitionSpec as P

F32, BF16 = jnp.float32, jnp.bfloat16
SLOT = 32
MID = 16
TILE = 256
NT = (((1,), (1,)), ((), ()))
NN = (((1,), (0,)), ((), ()))


def dot(a, b, dims):
    return lax.dot_general(a, b, dims, preferred_element_type=F32)


def layer_norm(values):
    shifted = values - jnp.mean(values, axis=-1, keepdims=True)
    variance = jnp.mean(shifted * shifted, axis=-1, keepdims=True)
    return (shifted * lax.rsqrt(variance + 1e-06)).astype(BF16)


def unit_rows(values):
    total = jnp.sum(values * values, axis=-1, keepdims=True)
    return (values * lax.rsqrt(total + 1e-06)).astype(BF16)


def kernel(
    cfg,
    scale_ref, shift_ref, ids_ref, tids_ref, x_ref, up_ref, down_ref, cap_ref, prior_ref,
    img_ref, txt_ref, *rest,
):
    n_pipe, n_dp, micros, rows, width, ff, texts, priors, spill = cfg
    if spill:
        eg, *rest = rest
    else:
        *rest, eg = rest
    (own, chunk, w_ref, ug, dg, xg, part, sc, rc, sz, rz, ma, ma2, mx, mx2, tp, tall,
     w_s, w_r, x_s, x_r, c_s, c_r, z_s, z_r, h_s, h_r, tp_s, tp_r, ta_s, ta_r,
     ea_s, ea_r, ez_s, ez_r, ey_s, ey_r, ex_s, ex_r, ec_s, ec_r, loc) = rest
    p, d = lax.axis_index("pipe"), lax.axis_index("dp")
    c, y, z = d % 2, (d // 2) % 2, d // 4
    zb, zp = z % 2, z // 2
    nz = n_dp // 4
    nzp = nz // 2
    groups = 2 * nzp
    last = n_pipe - 1
    oc, oz = 1 - c, 1 - zb

    def at(z_, y_, c_):
        return (z_ * 2 + y_) * 2 + c_

    d_c, d_y, d_z = at(z, y, oc), at(z, 1 - y, c), at(zp * 2 + oz, y, c)

    def copy(src, dst, s, r, pipe, dp):
        return pltpu.make_async_remote_copy(
            src_ref=src, dst_ref=dst, send_sem=s, recv_sem=r,
            device_id=(pipe, dp), device_id_type=pl.DeviceIdType.MESH)

    def arrived(dst, r):
        copy(dst, dst, loc.at[0], r, p, d_c).wait_recv()

    def left(src, s):
        copy(src, src, s, loc.at[0], p, d_c).wait_send()

    barrier = pltpu.get_barrier_semaphore()
    total = n_pipe * n_dp

    def greet(i, _):
        t = (p * n_dp + d + i) % total
        pl.semaphore_signal(barrier, inc=1, device_id=(t // n_dp, t % n_dp),
                            device_id_type=pl.DeviceIdType.MESH)
        return 0

    lax.fori_loop(1, total, greet, 0)

    own[...] = jnp.zeros_like(own)
    own[0:texts, :] = unit_rows(cap_ref[...].astype(F32))
    own[MID:MID + priors, :] = unit_rows(prior_ref[...])

    @pl.when(p == 0)
    def _():
        for m in range(micros):
            xg[zb, m, c] = x_ref[m]

    q = zp * 2 + y

    def wslot(ref, q_):
        return ref.at[pl.ds(pl.multiple_of(q_ * ff, 16), ff), :]

    shard = up_ref.shape[0]
    for k, (ref, given) in enumerate(((ug, up_ref), (dg, down_ref))):
        w_ref[k, 0:shard, :] = given[...]
        if ff > shard:
            w_ref[k, shard:ff, :] = jnp.zeros((ff - shard, width), BF16)
        ref[pl.ds(pl.multiple_of(q * ff, 16), ff), :] = w_ref[k]
    pl.semaphore_wait(barrier, total - 1)

    big = ((0, ug), (1, dg))

    def w_own_y(k, ref):
        return copy(w_ref.at[k], wslot(ref, q), w_s.at[k, 0], w_r.at[k, q], p, d_y)

    def w_own_z(k, ref, i):
        t = at(((zp + i) % nzp) * 2 + zb, y, c)
        return copy(w_ref.at[k], wslot(ref, q), w_s.at[k, i], w_r.at[k, q], p, t)

    def w_fwd(k, ref, i):
        q_ = ((zp + i) % nzp) * 2 + y
        return copy(wslot(ref, q_), wslot(ref, q_), w_s.at[k, nzp + i], w_r.at[k, q_], p, d_y)

    def x_c(m):
        return copy(xg.at[zb, m, c], xg.at[zb, m, c], x_s.at[0, m], x_r.at[zb, m, c], p, d_c)

    def x_z(m):
        return copy(xg.at[zb, m, c], xg.at[zb, m, c], x_s.at[1, m], x_r.at[zb, m, c], p, d_z)

    def x_f(m):
        return copy(xg.at[oz, m, c], xg.at[oz, m, c], x_s.at[2, m], x_r.at[oz, m, c], p, d_c)

    def w_start(k, ref):
        for i in range(1, nzp):
            w_own_z(k, ref, i).start()
        w_own_y(k, ref).start()

    def w_on(k, ref):
        for i in range(1, nzp):
            q_ = ((zp + i) % nzp) * 2 + y
            arrived(wslot(ref, q_), w_r.at[k, q_])
            w_fwd(k, ref, i).start()

    def w_here(k, ref):
        for i in range(nzp):
            q_ = ((zp + i) % nzp) * 2 + 1 - y
            arrived(wslot(ref, q_), w_r.at[k, q_])

    def eslot(index, count):
        return eg.at[pl.ds(index, count)]

    e_own = ((c * 2 + y) * nz + z) * n_pipe + p
    e_z, e_y, e_c = ((c * 2 + y) * nz + z) * n_pipe, (c * 2 + y) * nz * n_pipe, c * 2 * nz * n_pipe
    many = 2 * nz * n_pipe
    send_a = copy(own, eg.at[e_own], ea_s, ea_r.at[p], last, d)
    send_y = copy(eslot(e_y, nz * n_pipe), eslot(e_y, nz * n_pipe), ey_s, ey_r, p, d_y)
    send_c = copy(eslot(e_c, many), eslot(e_c, many), ec_s, ec_r, p, d_c)

    def send_z(i):
        return copy(eslot(e_z, n_pipe), eslot(e_z, n_pipe), ez_s.at[i], ez_r.at[z], p,
                    at((z + i) % nz, y, c))

    def send_x(i):
        return copy(eslot(e_c, many), eslot(e_c, many), ex_s.at[i], ex_r, (p + i) % n_pipe, d)

    def tokens_on():
        for m in range(micros):
            arrived(xg.at[oz, m, c], x_r.at[oz, m, c])
            x_f(m).start()

    def tokens_here():
        for m in range(micros):
            arrived(xg.at[zb, m, oc], x_r.at[zb, m, oc])
            arrived(xg.at[oz, m, oc], x_r.at[oz, m, oc])

    w_start(0, ug)

    @pl.when(p == 0)
    def _():
        for m in range(micros):
            x_c(m).start()
            x_z(m).start()

    @pl.when(p != last)
    def _():
        send_a.start()
        w_start(1, dg)
        w_on(0, ug)

    @pl.when(p == 0)
    def _():
        tokens_on()

    @pl.when(p == last)
    def _():
        keep = pltpu.make_async_copy(own, eg.at[e_own], loc.at[1])
        keep.start()
        keep.wait()
        for t in range(last):
            arrived(eg.at[e_z + t], ea_r.at[t])
        for i in range(1, nz):
            send_z(i).start()
        w_on(0, ug)
        w_start(1, dg)
        for i in range(1, nz):
            t = (z + i) % nz
            arrived(eslot(e_y + t * n_pipe, n_pipe), ez_r.at[t])
        send_y.start()
        w_on(1, dg)
        arrived(eslot((c * 2 + 1 - y) * nz * n_pipe, nz * n_pipe), ey_r)
        send_c.start()
        for i in range(1, n_pipe):
            send_x(i).start()
        w_here(0, ug)
        arrived(eslot(oc * many, many), ec_r)

    @pl.when(p != last)
    def _():
        w_on(1, dg)
        w_here(0, ug)

    if spill:
        ids_all, tids_all = ids_ref, tids_ref
    else:
        count = ids_ref.shape[1]
        square = (lax.broadcasted_iota(jnp.int32, (count, count), 0)
                  == lax.broadcasted_iota(jnp.int32, (count, count), 1))
        matches = jnp.max(jnp.where(square, ids_ref[...], -1), axis=1, keepdims=True)

        def look_up(index):
            shape = (count, index.shape[1])
            hit = lax.broadcasted_iota(jnp.int32, shape, 0) == index
            return jnp.max(jnp.where(hit, matches, -2), axis=0, keepdims=True)

        lane = lax.broadcasted_iota(jnp.int32, (1, total * SLOT), 1)
        s, r = lane // SLOT, lane % SLOT
        unit = s // n_pipe
        home = (s % n_pipe) * n_dp + ((unit % nz) * 2 + (unit // nz) % 2) * 2 + unit // (2 * nz)
        images = jnp.where((r >= MID) & (r < MID + priors), home * texts + 1 + r - MID, -1)
        ids_all = jnp.where(r < texts, home * texts + r, look_up(images))
        lane = lax.broadcasted_iota(jnp.int32, (1, 128), 1)
        m_, b_ = (lane // 2) % micros, (lane // (2 * micros)) % 2
        y_, z_ = (lane // (4 * micros)) % 2, lane // (8 * micros)
        home = m_ * n_dp + ((z_ * 2 + b_) * 2 + y_) * 2 + lane % 2
        tids_all = look_up(jnp.where(lane < tall.shape[0] * tall.shape[1], home * texts, -1))

    span = micros * 2 * rows
    tile = min(TILE, span)
    tiles = span // tile
    per = tile // rows
    mt = per // 2

    def activate(b, j):
        values = xg[b, pl.ds(j * mt, mt)].reshape(tile, width).astype(F32)
        act = jax.nn.gelu(dot(layer_norm(values), ug[...], NT), approximate=True)
        return values, act.astype(BF16)

    def hidden_out(m):
        return copy(sz.at[1, m], xg.at[zb, m, c], h_s.at[m], h_r.at[m],
                    jnp.minimum(p + 1, last), d)

    def to_core(b, m):
        return copy(sc.at[b, m], rc.at[b, m], c_s.at[b, m], c_r.at[b, m], p, d_c)

    def to_z(m):
        return copy(sz.at[0, m], rz.at[m], z_s.at[m], z_r.at[m], p, d_z)

    def take_hidden():
        for m in range(micros):
            arrived(xg.at[zb, m, c], h_r.at[m])
            x_c(m).start()
            x_z(m).start()
        tokens_on()

    @pl.when((p > 0) & (p < last))
    def _():
        take_hidden()

    @pl.when(p < last)
    def _():
        tokens_here()
        if tiles > 1:
            w_here(1, dg)
        for b in (oz, zb):
            def step(j, _, b=b):
                _, act = activate(b, j)
                if b is oz and tiles == 1:
                    w_here(1, dg)
                out = dot(act, dg[...], NN)
                part[b, pl.ds(j * mt, mt)] = out.reshape(mt, 2, rows, width)
                return 0

            if tiles == 1:
                step(0, 0)
            else:
                lax.fori_loop(0, tiles, step, 0)
            for m in range(micros):
                sc[b, m] = part[b, m, oc].astype(BF16)
                to_core(b, m).start()
            if b is oz:
                for m in range(micros):
                    arrived(rc.at[oz, m], c_r.at[oz, m])
                    sz[0, m] = (part[oz, m, c] + rc[oz, m].astype(F32)).astype(BF16)
                    to_z(m).start()
        for m in range(micros):
            arrived(rc.at[zb, m], c_r.at[zb, m])
            arrived(rz.at[m], z_r.at[m])
            new = part[zb, m, c] + rc[zb, m].astype(F32) + rz[m].astype(F32)
            sz[1, m] = (new + xg[zb, m, c].astype(F32)).astype(BF16)
            hidden_out(m).start()
        for m in range(micros):
            for b in range(2):
                left(sc.at[b, m], c_s.at[b, m])
            left(sz.at[0, m], z_s.at[m])
            left(sz.at[1, m], h_s.at[m])

        arrived(eslot(e_c, many), ex_r)
        send_c.start()
        arrived(eslot(oc * many, many), ec_r)

    scale, shift = scale_ref[0], shift_ref[0]
    n_rows = total * SLOT
    cs = chunk.shape[0] if spill else n_rows
    ids_w = n_rows

    def column(ref, first, count, limit):
        lane = lax.broadcasted_iota(jnp.int32, (count, limit), 1)
        row = lax.broadcasted_iota(jnp.int32, (count, limit), 0)
        return jnp.max(jnp.where(lane == row + first, ref[...], -1), axis=1, keepdims=True)

    def weigh(scores, row_ids, col_ids, keep_mask):
        logits = scale * scores + shift
        positive = row_ids == col_ids
        w = jnp.where(positive, -scale * jax.nn.sigmoid(-logits), scale * jax.nn.sigmoid(logits))
        return jnp.where(keep_mask, w, 0.0).astype(BF16)

    def block(j):
        if not spill:
            return eg[...].reshape(n_rows, width), ids_all
        fetch = pltpu.make_async_copy(eg.at[pl.ds(j * (cs // SLOT), cs // SLOT)], chunk2, loc.at[1])
        fetch.start()
        fetch.wait()
        return chunk2[...].reshape(cs, width), ids_all[:, pl.ds(pl.multiple_of(j * cs, cs), cs)]

    chunk2 = chunk.reshape(cs // SLOT, SLOT, width) if spill else None
    own_v = own[...]
    own_ids = column(ids_all, e_own * SLOT, SLOT, ids_w)
    kind_r = lax.broadcasted_iota(jnp.int32, (SLOT, cs), 0)
    kind_c = lax.broadcasted_iota(jnp.int32, (SLOT, cs), 1) % SLOT
    text_c = kind_c < texts
    prior_c = (kind_c >= MID) & (kind_c < MID + priors)
    mask = ((kind_r < texts) & prior_c) | ((kind_r >= MID) & text_c)

    def early(j, acc):
        e, ids = block(j)
        w = weigh(dot(own_v, e, NT), own_ids, ids, mask)
        return acc + dot(w, e, NN)

    if spill:
        grads = lax.fori_loop(0, n_rows // cs, early, jnp.zeros((SLOT, width), F32))
    else:
        grads = early(0, 0.0)
    img_ref[1:1 + priors, :] = grads[MID:MID + priors]

    @pl.when(p == last)
    def _():
        def step(i, _):
            b, j = i // tiles, i % tiles
            values, act = activate(b, j)
            ma[i] = jnp.mean(act.astype(F32).reshape(per, rows, -1), axis=1)
            mx[i] = jnp.mean(values.reshape(per, rows, width), axis=1)
            return 0

        take_hidden()
        tokens_here()
        lax.fori_loop(0, 2 * tiles, step, 0)
        w_here(1, dg)
        for i in range(2 * tiles):
            ma2[i * per:(i + 1) * per, :] = ma[i]
            mx2[i * per:(i + 1) * per, :] = mx[i]
        t = zb * 2 + c
        tp[t] = dot(ma2[...].astype(BF16), dg[...], NN)

        def t_out(i):
            t_ = (t + i) % 4
            return copy(tp.at[t], tp.at[t], tp_s.at[i], tp_r.at[t], p,
                        at(zp * 2 + t_ // 2, y, t_ % 2))

        for i in range(1, 4):
            t_out(i).start()
        for i in range(1, 4):
            t_ = (t + i) % 4
            arrived(tp.at[t_], tp_r.at[t_])
        pooled = mx2[...] + (tp[0] + tp[1]) + (tp[2] + tp[3])
        tall[q] = unit_rows(pooled).astype(F32)

        def spread(i, _):
            s = (last * groups + q + i) % (n_pipe * groups)
            g = s % groups
            copy(tall.at[q], tall.at[q], ta_s.at[i], ta_r.at[q], s // groups,
                 at((g // 2) * 2 + zb, g % 2, c)).start()
            return 0

        lax.fori_loop(1, n_pipe * groups, spread, 0)
        for i in range(1, 4):
            left(tp.at[t], tp_s.at[i])
        for i in range(1, groups):
            g = (q + i) % groups
            arrived(tall.at[g], ta_r.at[g])
        for i in range(1, n_pipe * groups):
            left(tall.at[q], ta_s.at[i])

    @pl.when(p != last)
    def _():
        for g in range(groups):
            arrived(tall.at[g], ta_r.at[g])

    n_t = tall.shape[0] * tall.shape[1]
    towers = tall[...].reshape(n_t, width).astype(BF16)
    t_ids = tids_all[...][:, :n_t]
    rmask = lax.broadcasted_iota(jnp.int32, (SLOT, n_t), 0) < texts
    w = weigh(dot(own_v, towers, NT), own_ids, t_ids, rmask)
    txt_ref[...] = (grads + dot(w, towers, NN))[:texts]

    mine = (zb * micros + p) * 2 + c
    pick = lax.broadcasted_iota(jnp.int32, (tall.shape[1], width), 0) == mine
    row = jnp.sum(jnp.where(pick, tall[q], 0.0), axis=0, keepdims=True)
    row8 = jnp.broadcast_to(row, (8, width)).astype(BF16)
    row_id = column(tids_all, q * tall.shape[1] + mine, 1, tids_all.shape[1])
    row_ids = jnp.broadcast_to(row_id, (8, 1))

    def late(j, acc):
        e, ids = block(j)
        w = weigh(dot(row8, e, NT), row_ids, ids, text_c[:8])
        return acc + dot(w, e, NN)

    if spill:
        g_row = lax.fori_loop(0, n_rows // cs, late, jnp.zeros((8, width), F32))
    else:
        g_row = late(0, 0.0)
    img_ref[0:1, :] = g_row[0:1]

    for k, ref in big:
        for i in range(nzp):
            left(w_ref.at[k], w_s.at[k, i])
        for i in range(1, nzp):
            left(w_ref.at[k], w_s.at[k, nzp + i])
    for m in range(micros):
        for i in range(3):
            left(xg.at[zb, m, c], x_s.at[i, m])
    send_c.wait_send()

    @pl.when(p == last)
    def _():
        for i in range(1, nz):
            left(eslot(e_z, n_pipe), ez_s.at[i])
        send_y.wait_send()
        for i in range(1, n_pipe):
            left(eslot(e_c, many), ex_s.at[i])

    @pl.when(p != last)
    def _():
        send_a.wait_send()


def id_rows(match, n_pipe, nz, texts, priors):
    total = n_pipe * nz * 4

    def placed(numbers):
        numbers = numbers.reshape(n_pipe, nz, 2, 2, texts)
        return numbers.transpose(3, 2, 1, 0, 4).reshape(total, texts)

    ids = jnp.concatenate([
        jnp.pad(placed(jnp.arange(total * texts, dtype=jnp.int32)),
                ((0, 0), (0, MID - texts)), constant_values=-2),
        jnp.pad(placed(match)[:, 1:], ((0, 0), (0, SLOT - MID - priors)), constant_values=-2),
    ], axis=1).reshape(1, total * SLOT)
    tids = match.reshape(n_pipe, nz // 2, 2, 2, 2, texts)[..., 0]
    tids = tids.transpose(1, 3, 2, 0, 4).reshape(1, -1)
    tids = jnp.pad(tids, ((0, 0), (0, -tids.shape[1] % 128)), constant_values=-2)
    return ids, tids


def body(vis, up, down, cap, prior, match, scale, shift):
    n_pipe, n_dp = lax.axis_size("pipe"), lax.axis_size("dp")
    micros, img_mb, patch, width = vis.shape
    rows = img_mb * patch
    shard = up.shape[2]
    ff = -(-shard // 16) * 16
    texts, priors = cap.shape[0], prior.shape[0]
    nz, total = n_dp // 4, n_pipe * n_dp
    nzp = nz // 2
    groups = 2 * nzp
    spill = total > 64
    if spill:
        ids, tids = id_rows(match, n_pipe, nz, texts, priors)
    else:
        ids = tids = match.reshape(1, -1)
    cfg = (n_pipe, n_dp, micros, rows, width, ff, texts, priors, spill)
    span = micros * 2 * rows
    tile = min(TILE, span)
    tiles, kept = span // tile, tile // rows
    imgs = 4 * micros
    ffg = groups * ff
    vm = pl.BlockSpec(memory_space=pltpu.VMEM)
    sm = pl.BlockSpec(memory_space=pltpu.SMEM)
    dma = pltpu.SemaphoreType.DMA
    outs = [jax.ShapeDtypeStruct((texts, width), F32)] * 2
    out_specs = [vm, vm]
    eg_shape = (total, SLOT, width)
    scratch = [
        pltpu.VMEM((SLOT, width), BF16),
        pltpu.VMEM((1024, width) if spill else (16, width), BF16),
        pltpu.VMEM((2, ff, width), BF16),
        pltpu.VMEM((ffg, width), BF16),
        pltpu.VMEM((ffg, width), BF16),
        pltpu.VMEM((2, micros, 2, rows, width), BF16),
        pltpu.VMEM((2, micros, 2, rows, width), F32),
        pltpu.VMEM((2, micros, rows, width), BF16),
        pltpu.VMEM((2, micros, rows, width), BF16),
        pltpu.VMEM((2, micros, rows, width), BF16),
        pltpu.VMEM((micros, rows, width), BF16),
        pltpu.VMEM((2 * tiles, kept, ffg), F32),
        pltpu.VMEM((imgs, ffg), F32),
        pltpu.VMEM((2 * tiles, kept, width), F32),
        pltpu.VMEM((imgs, width), F32),
        pltpu.VMEM((4, imgs, width), F32),
        pltpu.VMEM((groups, imgs, width), F32),
        dma((2, 2 * nzp)), dma((2, groups)),
        dma((3, micros)), dma((2, micros, 2)),
        dma((2, micros)), dma((2, micros)),
        dma((micros,)), dma((micros,)),
        dma((micros,)), dma((micros,)),
        dma((4,)), dma((4,)),
        dma((n_pipe * groups,)), dma((groups,)),
        dma, dma((n_pipe,)),
        dma((nz,)), dma((nz,)),
        dma, dma,
        dma((n_pipe,)), dma,
        dma, dma,
        dma((2,)),
    ]
    if spill:
        outs = outs + [jax.ShapeDtypeStruct(eg_shape, BF16)]
        out_specs = out_specs + [pl.BlockSpec(memory_space=pl.ANY)]
    else:
        scratch = scratch + [pltpu.VMEM(eg_shape, BF16)]
    result = pl.pallas_call(
        functools.partial(kernel, cfg),
        out_shape=outs,
        in_specs=[sm, sm, vm, vm, vm, vm, vm, vm, vm],
        out_specs=out_specs,
        scratch_shapes=scratch,
        compiler_params=pltpu.CompilerParams(
            collective_id=0, has_side_effects=True, vmem_limit_bytes=60 * 2**20),
    )(scale, shift, ids, tids, vis.reshape(micros, rows, width), up[0].T, down[0], cap, prior)
    return result[0], result[1]


def solution(mesh):
    placed = (
        P(None, "dp", None, None),
        P("pipe", None, "dp"),
        P("pipe", "dp", None),
        P(("pipe", "dp"), None),
        P(("pipe", "dp"), None),
        P(),
        P(),
        P(),
    )
    return jax.shard_map(
        body,
        mesh=mesh,
        in_specs=placed,
        out_specs=(P(("pipe", "dp"), None), P(("pipe", "dp"), None)),
        check_vma=False,
    )
```

```python
import functools

import jax
import jax.numpy as jnp
from jax import lax
from jax.experimental import pallas as pl
from jax.experimental.pallas import tpu as pltpu
from jax.sharding import PartitionSpec as P

F32, BF16 = jnp.float32, jnp.bfloat16
SLOT = 32
MID = 16
TILE = 256
NT = (((1,), (1,)), ((), ()))
NN = (((1,), (0,)), ((), ()))


def dot(a, b, dims):
    return lax.dot_general(a, b, dims, preferred_element_type=F32)


def layer_norm(values):
    shifted = values - jnp.mean(values, axis=-1, keepdims=True)
    variance = jnp.mean(shifted * shifted, axis=-1, keepdims=True)
    return (shifted * lax.rsqrt(variance + 1e-06)).astype(BF16)


def unit_rows(values):
    total = jnp.sum(values * values, axis=-1, keepdims=True)
    return (values * lax.rsqrt(total + 1e-06)).astype(BF16)


def kernel(
    cfg,
    scale_ref, shift_ref, ids_ref, tids_ref, x_ref, up_ref, down_ref, cap_ref, prior_ref,
    img_ref, txt_ref, *rest,
):
    n_pipe, n_dp, micros, rows, width, ff, texts, priors, spill = cfg
    if spill:
        eg, *rest = rest
    else:
        *rest, eg = rest
    (own, chunk, w_ref, ul, dl, xl, rx, ug, dg, xg, part, sc, rc, sz, rz, ma, ma2, mx, mx2, tp, tall,
     w_s, w_r, x_s, x_r, c_s, c_r, z_s, z_r, h_s, h_r, tp_s, tp_r, ta_s, ta_r,
     ea_s, ea_r, ez_s, ez_r, ey_s, ey_r, ex_s, ex_r, ec_s, ec_r,
     hw_s, hw_r, hx_s, hx_r, xl_s, xl_r, loc) = rest
    p, d = lax.axis_index("pipe"), lax.axis_index("dp")
    c, y, z = d % 2, (d // 2) % 2, d // 4
    zb, zp = z % 2, z // 2
    nz = n_dp // 4
    nzp = nz // 2
    groups = 2 * nzp
    last = n_pipe - 1
    oc, oz = 1 - c, 1 - zb

    def at(z_, y_, c_):
        return (z_ * 2 + y_) * 2 + c_

    d_c, d_y, d_z = at(z, y, oc), at(z, 1 - y, c), at(zp * 2 + oz, y, c)

    def copy(src, dst, s, r, pipe, dp):
        return pltpu.make_async_remote_copy(
            src_ref=src, dst_ref=dst, send_sem=s, recv_sem=r,
            device_id=(pipe, dp), device_id_type=pl.DeviceIdType.MESH)

    def arrived(dst, r):
        copy(dst, dst, loc.at[0], r, p, d_c).wait_recv()

    def left(src, s):
        copy(src, src, s, loc.at[0], p, d_c).wait_send()

    barrier = pltpu.get_barrier_semaphore()
    total = n_pipe * n_dp

    def greet(i, _):
        t = (p * n_dp + d + i) % total
        pl.semaphore_signal(barrier, inc=1, device_id=(t // n_dp, t % n_dp),
                            device_id_type=pl.DeviceIdType.MESH)
        return 0

    lax.fori_loop(1, total, greet, 0)

    own[...] = jnp.zeros_like(own)
    own[0:texts, :] = unit_rows(cap_ref[...].astype(F32))
    own[MID:MID + priors, :] = unit_rows(prior_ref[...])

    @pl.when(p <= 1)
    def _():
        for m in range(micros):
            xl[zb, m, c] = x_ref[m]

    q = zp * 2 + y

    def wslot(ref, q_):
        return ref.at[pl.ds(pl.multiple_of(q_ * ff, 16), ff), :]

    shard = up_ref.shape[0]
    half = ul.shape[0] // groups
    for k, (ref, given) in enumerate(((ug, up_ref), (dg, down_ref))):
        w_ref[k, 0:shard, :] = given[...]
        if 2 * half > shard:
            w_ref[k, shard:2 * half, :] = jnp.zeros((2 * half - shard, width), BF16)
        ref[pl.ds(pl.multiple_of(q * ff, 16), ff), :] = w_ref[k, 0:ff, :]

    @pl.when(p == 0)
    def _():
        for k, ref in enumerate((ul, dl)):
            ref[pl.ds(pl.multiple_of(q * half, 16), half), :] = w_ref[k, 0:half, :]
    pl.semaphore_wait(barrier, total - 1)

    big = ((0, ug), (1, dg))

    def w_own_y(k, ref):
        return copy(w_ref.at[k, pl.ds(0, ff)], wslot(ref, q), w_s.at[k, 0], w_r.at[k, q], p, d_y)

    def w_own_z(k, ref, i):
        t = at(((zp + i) % nzp) * 2 + zb, y, c)
        return copy(w_ref.at[k, pl.ds(0, ff)], wslot(ref, q), w_s.at[k, i], w_r.at[k, q], p, t)

    def w_fwd(k, ref, i):
        q_ = ((zp + i) % nzp) * 2 + y
        return copy(wslot(ref, q_), wslot(ref, q_), w_s.at[k, nzp + i], w_r.at[k, q_], p, d_y)

    def x_c(buf, ss, rr, m):
        return copy(buf.at[zb, m, c], buf.at[zb, m, c], ss.at[0, m], rr.at[zb, m, c], p, d_c)

    def x_z(buf, ss, rr, m):
        return copy(buf.at[zb, m, c], buf.at[zb, m, c], ss.at[1, m], rr.at[zb, m, c], p, d_z)

    def x_f(buf, ss, rr, m):
        return copy(buf.at[oz, m, c], buf.at[oz, m, c], ss.at[2, m], rr.at[oz, m, c], p, d_c)

    def hslot(ref, q_):
        return ref.at[pl.ds(pl.multiple_of(q_ * half, 16), half), :]

    halves = ((0, ul), (1, dl))

    def h_over(k, ref):
        return copy(w_ref.at[k, pl.ds(half, half)], hslot(ref, q), hx_s.at[k], hx_r.at[k], 1, d)

    def h_start(k, ref):
        for i in range(1, nzp):
            t = at(((zp + i) % nzp) * 2 + zb, y, c)
            copy(hslot(ref, q), hslot(ref, q), hw_s.at[k, i], hw_r.at[k, q], p, t).start()
        copy(hslot(ref, q), hslot(ref, q), hw_s.at[k, 0], hw_r.at[k, q], p, d_y).start()

    def h_on(k, ref):
        for i in range(1, nzp):
            q_ = ((zp + i) % nzp) * 2 + y
            arrived(hslot(ref, q_), hw_r.at[k, q_])
            copy(hslot(ref, q_), hslot(ref, q_), hw_s.at[k, nzp + i], hw_r.at[k, q_], p, d_y).start()

    def h_here(k, ref):
        for i in range(nzp):
            q_ = ((zp + i) % nzp) * 2 + 1 - y
            arrived(hslot(ref, q_), hw_r.at[k, q_])

    def w_start(k, ref):
        for i in range(1, nzp):
            w_own_z(k, ref, i).start()
        w_own_y(k, ref).start()

    def w_on(k, ref):
        for i in range(1, nzp):
            q_ = ((zp + i) % nzp) * 2 + y
            arrived(wslot(ref, q_), w_r.at[k, q_])
            w_fwd(k, ref, i).start()

    def w_here(k, ref):
        for i in range(nzp):
            q_ = ((zp + i) % nzp) * 2 + 1 - y
            arrived(wslot(ref, q_), w_r.at[k, q_])

    def eslot(index, count):
        return eg.at[pl.ds(index, count)]

    e_own = ((c * 2 + y) * nz + z) * n_pipe + p
    e_z, e_y, e_c = ((c * 2 + y) * nz + z) * n_pipe, (c * 2 + y) * nz * n_pipe, c * 2 * nz * n_pipe
    many = 2 * nz * n_pipe
    send_a = copy(own, eg.at[e_own], ea_s, ea_r.at[p], last, d)
    send_y = copy(eslot(e_y, nz * n_pipe), eslot(e_y, nz * n_pipe), ey_s, ey_r, p, d_y)
    send_c = copy(eslot(e_c, many), eslot(e_c, many), ec_s, ec_r, p, d_c)

    def send_z(i):
        return copy(eslot(e_z, n_pipe), eslot(e_z, n_pipe), ez_s.at[i], ez_r.at[z], p,
                    at((z + i) % nz, y, c))

    def send_x(i):
        return copy(eslot(e_c, many), eslot(e_c, many), ex_s.at[i], ex_r, (p + i) % n_pipe, d)

    def tokens_out(buf, ss, rr, m):
        x_c(buf, ss, rr, m).start()
        x_z(buf, ss, rr, m).start()

    def tokens_on(buf, ss, rr):
        for m in range(micros):
            arrived(buf.at[oz, m, c], rr.at[oz, m, c])
            x_f(buf, ss, rr, m).start()

    def tokens_here(buf, rr):
        for m in range(micros):
            arrived(buf.at[zb, m, oc], rr.at[zb, m, oc])
            arrived(buf.at[oz, m, oc], rr.at[oz, m, oc])

    def emb_start():
        keep = pltpu.make_async_copy(own, eg.at[e_own], loc.at[1])
        keep.start()
        keep.wait()
        for t in range(last):
            arrived(eg.at[e_z + t], ea_r.at[t])
        for i in range(1, nz):
            send_z(i).start()

    def emb_middle():
        for i in range(1, nz):
            t = (z + i) % nz
            arrived(eslot(e_y + t * n_pipe, n_pipe), ez_r.at[t])
        send_y.start()

    def emb_end():
        arrived(eslot((c * 2 + 1 - y) * nz * n_pipe, nz * n_pipe), ey_r)
        send_c.start()
        for i in range(1, n_pipe):
            send_x(i).start()

    lx = (xl, xl_s, xl_r)
    gx = (xg, x_s, x_r)

    @pl.when(p != last)
    def _():
        send_a.start()

    @pl.when(p == 0)
    def _():
        h_over(0, ul).start()
        h_start(0, ul)
        h_over(1, dl).start()
        h_start(1, dl)
        for m in range(micros):
            tokens_out(*lx, m)
        h_on(0, ul)
        h_on(1, dl)

    @pl.when(p == 1)
    def _():
        for m in range(micros):
            tokens_out(*lx, m)
        arrived(hslot(ul, q), hx_r.at[0])
        h_start(0, ul)
        arrived(hslot(dl, q), hx_r.at[1])
        h_start(1, dl)
        h_on(0, ul)
        h_on(1, dl)

    @pl.when(p <= 1)
    def _():
        tokens_on(*lx)

    @pl.when(p > 0)
    def _():
        w_start(0, ug)

    @pl.when(p == last)
    def _():
        emb_start()

    if spill:
        ids_all, tids_all = ids_ref, tids_ref
    else:
        count = ids_ref.shape[1]
        square = (lax.broadcasted_iota(jnp.int32, (count, count), 0)
                  == lax.broadcasted_iota(jnp.int32, (count, count), 1))
        matches = jnp.max(jnp.where(square, ids_ref[...], -1), axis=1, keepdims=True)

        def look_up(index):
            shape = (count, index.shape[1])
            hit = lax.broadcasted_iota(jnp.int32, shape, 0) == index
            return jnp.max(jnp.where(hit, matches, -2), axis=0, keepdims=True)

        lane = lax.broadcasted_iota(jnp.int32, (1, total * SLOT), 1)
        s, r = lane // SLOT, lane % SLOT
        unit = s // n_pipe
        home = (s % n_pipe) * n_dp + ((unit % nz) * 2 + (unit // nz) % 2) * 2 + unit // (2 * nz)
        images = jnp.where((r >= MID) & (r < MID + priors), home * texts + 1 + r - MID, -1)
        ids_all = jnp.where(r < texts, home * texts + r, look_up(images))
        lane = lax.broadcasted_iota(jnp.int32, (1, 128), 1)
        m_, b_ = (lane // 2) % micros, (lane // (2 * micros)) % 2
        y_, z_ = (lane // (4 * micros)) % 2, lane // (8 * micros)
        home = m_ * n_dp + ((z_ * 2 + b_) * 2 + y_) * 2 + lane % 2
        tids_all = look_up(jnp.where(lane < tall.shape[0] * tall.shape[1], home * texts, -1))

    span = micros * 2 * rows
    tile = min(TILE, span)
    tiles = span // tile
    per = tile // rows
    mt = per // 2

    def activate(buf, u, b, j):
        values = buf[b, pl.ds(j * mt, mt)].reshape(tile, width).astype(F32)
        act = jax.nn.gelu(dot(layer_norm(values), u[...], NT), approximate=True)
        return values, act.astype(BF16)

    def to_core(b, m):
        return copy(sc.at[b, m], rc.at[b, m], c_s.at[b, m], c_r.at[b, m], p, d_c)

    def to_z(m):
        return copy(sz.at[0, m], rz.at[m], z_s.at[m], z_r.at[m], p, d_z)

    def reduce_rows(buf, u, dn, await_dn, between, emit):
        for first, b in ((True, oz), (False, zb)):
            def step(j, _, first=first, b=b):
                _, act = activate(buf, u, b, j)
                if first and tiles == 1:
                    await_dn()
                part[b, pl.ds(j * mt, mt)] = dot(act, dn[...], NN).reshape(mt, 2, rows, width)
                return 0

            if tiles == 1:
                step(0, 0)
            else:
                if first:
                    await_dn()
                lax.fori_loop(0, tiles, step, 0)
            for m in range(micros):
                sc[b, m] = part[b, m, oc].astype(BF16)
                to_core(b, m).start()
            if first:
                for m in range(micros):
                    arrived(rc.at[oz, m], c_r.at[oz, m])
                    sz[0, m] = (part[oz, m, c] + rc[oz, m].astype(F32)).astype(BF16)
                    to_z(m).start()
        between()
        for m in range(micros):
            arrived(rc.at[zb, m], c_r.at[zb, m])
            arrived(rz.at[m], z_r.at[m])
            emit(m, part[zb, m, c] + rc[zb, m].astype(F32) + rz[m].astype(F32))
        for m in range(micros):
            for b in range(2):
                left(sc.at[b, m], c_s.at[b, m])
            left(sz.at[0, m], z_s.at[m])

    def to_rx(m):
        return copy(sz.at[1, m], rx.at[m], h_s.at[m], h_r.at[m], 1, d)

    def hidden_out(m):
        return copy(sz.at[1, m], xg.at[zb, m, c], h_s.at[m], h_r.at[m],
                    jnp.minimum(p + 1, last), d)

    @pl.when(p <= 1)
    def _():
        h_here(0, ul)
        tokens_here(xl, xl_r)

        def await_dl():
            h_here(1, dl)

        def between():
            @pl.when(p == 1)
            def _():
                w_on(0, ug)
                w_start(1, dg)

            @pl.when(p == last)
            def _():
                emb_middle()

        def emit(m, value):
            @pl.when(p == 0)
            def _():
                sz[1, m] = value.astype(BF16)
                to_rx(m).start()

            @pl.when(p == 1)
            def _():
                arrived(rx.at[m], h_r.at[m])
                new = value + rx[m].astype(F32) + xl[zb, m, c].astype(F32)
                xg[zb, m, c] = new.astype(BF16)
                tokens_out(*gx, m)

        reduce_rows(xl, ul, dl, await_dl, between, emit)

    def take_hidden():
        for m in range(micros):
            arrived(xg.at[zb, m, c], h_r.at[m])
            tokens_out(*gx, m)

    if n_pipe > 2:
        @pl.when(p > 1)
        def _():
            w_start(1, dg)
            w_on(0, ug)

        @pl.when((p > 0) & (p < last))
        def _():
            @pl.when(p > 1)
            def _():
                take_hidden()

            tokens_on(*gx)
            w_on(1, dg)
            w_here(0, ug)
            tokens_here(xg, x_r)

            def emit(m, value):
                sz[1, m] = (value + xg[zb, m, c].astype(F32)).astype(BF16)
                hidden_out(m).start()

            reduce_rows(xg, ug, dg, lambda: w_here(1, dg), lambda: None, emit)

        @pl.when(p == last)
        def _():
            emb_middle()

    @pl.when(p == last)
    def _():
        emb_end()
        if n_pipe == 2:
            tokens_on(*gx)
        w_on(1, dg)
        w_here(0, ug)
        arrived(eslot(oc * many, many), ec_r)

    @pl.when(p != last)
    def _():
        for m in range(micros):
            left(sz.at[1, m], h_s.at[m])
        arrived(eslot(e_c, many), ex_r)
        send_c.start()
        arrived(eslot(oc * many, many), ec_r)

    scale, shift = scale_ref[0], shift_ref[0]
    n_rows = total * SLOT
    cs = chunk.shape[0] if spill else n_rows
    ids_w = n_rows

    def column(ref, first, count, limit):
        lane = lax.broadcasted_iota(jnp.int32, (count, limit), 1)
        row = lax.broadcasted_iota(jnp.int32, (count, limit), 0)
        return jnp.max(jnp.where(lane == row + first, ref[...], -1), axis=1, keepdims=True)

    def weigh(scores, row_ids, col_ids, keep_mask):
        logits = scale * scores + shift
        positive = row_ids == col_ids
        w = jnp.where(positive, -scale * jax.nn.sigmoid(-logits), scale * jax.nn.sigmoid(logits))
        return jnp.where(keep_mask, w, 0.0).astype(BF16)

    def block(j):
        if not spill:
            return eg[...].reshape(n_rows, width), ids_all
        fetch = pltpu.make_async_copy(eg.at[pl.ds(j * (cs // SLOT), cs // SLOT)], chunk2, loc.at[1])
        fetch.start()
        fetch.wait()
        return chunk2[...].reshape(cs, width), ids_all[:, pl.ds(pl.multiple_of(j * cs, cs), cs)]

    chunk2 = chunk.reshape(cs // SLOT, SLOT, width) if spill else None
    own_v = own[...]
    own_ids = column(ids_all, e_own * SLOT, SLOT, ids_w)
    kind_r = lax.broadcasted_iota(jnp.int32, (SLOT, cs), 0)
    kind_c = lax.broadcasted_iota(jnp.int32, (SLOT, cs), 1) % SLOT
    text_c = kind_c < texts
    prior_c = (kind_c >= MID) & (kind_c < MID + priors)
    mask = ((kind_r < texts) & prior_c) | ((kind_r >= MID) & text_c)

    def early(j, acc):
        e, ids = block(j)
        w = weigh(dot(own_v, e, NT), own_ids, ids, mask)
        return acc + dot(w, e, NN)

    if spill:
        grads = lax.fori_loop(0, n_rows // cs, early, jnp.zeros((SLOT, width), F32))
    else:
        grads = early(0, 0.0)
    img_ref[1:1 + priors, :] = grads[MID:MID + priors]

    @pl.when(p == last)
    def _():
        def step(i, _):
            b, j = i // tiles, i % tiles
            values, act = activate(xg, ug, b, j)
            ma[i] = jnp.mean(act.astype(F32).reshape(per, rows, -1), axis=1)
            mx[i] = jnp.mean(values.reshape(per, rows, width), axis=1)
            return 0

        if n_pipe > 2:
            take_hidden()
            tokens_on(*gx)
        tokens_here(xg, x_r)
        lax.fori_loop(0, 2 * tiles, step, 0)
        w_here(1, dg)
        for i in range(2 * tiles):
            ma2[i * per:(i + 1) * per, :] = ma[i]
            mx2[i * per:(i + 1) * per, :] = mx[i]
        t = zb * 2 + c
        tp[t] = dot(ma2[...].astype(BF16), dg[...], NN)

        def t_out(i):
            t_ = (t + i) % 4
            return copy(tp.at[t], tp.at[t], tp_s.at[i], tp_r.at[t], p,
                        at(zp * 2 + t_ // 2, y, t_ % 2))

        for i in range(1, 4):
            t_out(i).start()
        for i in range(1, 4):
            t_ = (t + i) % 4
            arrived(tp.at[t_], tp_r.at[t_])
        pooled = mx2[...] + (tp[0] + tp[1]) + (tp[2] + tp[3])
        tall[q] = unit_rows(pooled).astype(F32)

        def spread(i, _):
            s = (last * groups + q + i) % (n_pipe * groups)
            g = s % groups
            copy(tall.at[q], tall.at[q], ta_s.at[i], ta_r.at[q], s // groups,
                 at((g // 2) * 2 + zb, g % 2, c)).start()
            return 0

        lax.fori_loop(1, n_pipe * groups, spread, 0)
        for i in range(1, 4):
            left(tp.at[t], tp_s.at[i])
        for i in range(1, groups):
            g = (q + i) % groups
            arrived(tall.at[g], ta_r.at[g])
        for i in range(1, n_pipe * groups):
            left(tall.at[q], ta_s.at[i])

    @pl.when(p != last)
    def _():
        for g in range(groups):
            arrived(tall.at[g], ta_r.at[g])

    n_t = tall.shape[0] * tall.shape[1]
    towers = tall[...].reshape(n_t, width).astype(BF16)
    t_ids = tids_all[...][:, :n_t]
    rmask = lax.broadcasted_iota(jnp.int32, (SLOT, n_t), 0) < texts
    w = weigh(dot(own_v, towers, NT), own_ids, t_ids, rmask)
    txt_ref[...] = (grads + dot(w, towers, NN))[:texts]

    mine = (zb * micros + p) * 2 + c
    pick = lax.broadcasted_iota(jnp.int32, (tall.shape[1], width), 0) == mine
    row = jnp.sum(jnp.where(pick, tall[q], 0.0), axis=0, keepdims=True)
    row8 = jnp.broadcast_to(row, (8, width)).astype(BF16)
    row_id = column(tids_all, q * tall.shape[1] + mine, 1, tids_all.shape[1])
    row_ids = jnp.broadcast_to(row_id, (8, 1))

    def late(j, acc):
        e, ids = block(j)
        w = weigh(dot(row8, e, NT), row_ids, ids, text_c[:8])
        return acc + dot(w, e, NN)

    if spill:
        g_row = lax.fori_loop(0, n_rows // cs, late, jnp.zeros((8, width), F32))
    else:
        g_row = late(0, 0.0)
    img_ref[0:1, :] = g_row[0:1]

    @pl.when(p > 0)
    def _():
        for k, ref in big:
            for i in range(nzp):
                left(w_ref.at[k, pl.ds(0, ff)], w_s.at[k, i])
            for i in range(1, nzp):
                left(w_ref.at[k, pl.ds(0, ff)], w_s.at[k, nzp + i])
        for m in range(micros):
            for i in range(3):
                left(xg.at[zb, m, c], x_s.at[i, m])

    @pl.when(p == 0)
    def _():
        for k in range(2):
            left(w_ref.at[k, pl.ds(half, half)], hx_s.at[k])

    @pl.when(p <= 1)
    def _():
        for k, ref in halves:
            for i in range(nzp):
                left(hslot(ref, q), hw_s.at[k, i])
            for i in range(1, nzp):
                left(hslot(ref, q), hw_s.at[k, nzp + i])
        for m in range(micros):
            for i in range(3):
                left(xl.at[zb, m, c], xl_s.at[i, m])

    send_c.wait_send()

    @pl.when(p == last)
    def _():
        for i in range(1, nz):
            left(eslot(e_z, n_pipe), ez_s.at[i])
        send_y.wait_send()
        for i in range(1, n_pipe):
            left(eslot(e_c, many), ex_s.at[i])

    @pl.when(p != last)
    def _():
        send_a.wait_send()


def id_rows(match, n_pipe, nz, texts, priors):
    total = n_pipe * nz * 4

    def placed(numbers):
        numbers = numbers.reshape(n_pipe, nz, 2, 2, texts)
        return numbers.transpose(3, 2, 1, 0, 4).reshape(total, texts)

    ids = jnp.concatenate([
        jnp.pad(placed(jnp.arange(total * texts, dtype=jnp.int32)),
                ((0, 0), (0, MID - texts)), constant_values=-2),
        jnp.pad(placed(match)[:, 1:], ((0, 0), (0, SLOT - MID - priors)), constant_values=-2),
    ], axis=1).reshape(1, total * SLOT)
    tids = match.reshape(n_pipe, nz // 2, 2, 2, 2, texts)[..., 0]
    tids = tids.transpose(1, 3, 2, 0, 4).reshape(1, -1)
    tids = jnp.pad(tids, ((0, 0), (0, -tids.shape[1] % 128)), constant_values=-2)
    return ids, tids


def body(vis, up, down, cap, prior, match, scale, shift):
    n_pipe, n_dp = lax.axis_size("pipe"), lax.axis_size("dp")
    micros, img_mb, patch, width = vis.shape
    rows = img_mb * patch
    shard = up.shape[2]
    ff = -(-shard // 16) * 16
    texts, priors = cap.shape[0], prior.shape[0]
    nz, total = n_dp // 4, n_pipe * n_dp
    nzp = nz // 2
    groups = 2 * nzp
    spill = total > 64
    if spill:
        ids, tids = id_rows(match, n_pipe, nz, texts, priors)
    else:
        ids = tids = match.reshape(1, -1)
    cfg = (n_pipe, n_dp, micros, rows, width, ff, texts, priors, spill)
    span = micros * 2 * rows
    tile = min(TILE, span)
    tiles, kept = span // tile, tile // rows
    imgs = 4 * micros
    ffg = groups * ff
    half = -(-ff // 32) * 16
    vm = pl.BlockSpec(memory_space=pltpu.VMEM)
    sm = pl.BlockSpec(memory_space=pltpu.SMEM)
    dma = pltpu.SemaphoreType.DMA
    outs = [jax.ShapeDtypeStruct((texts, width), F32)] * 2
    out_specs = [vm, vm]
    eg_shape = (total, SLOT, width)
    scratch = [
        pltpu.VMEM((SLOT, width), BF16),
        pltpu.VMEM((1024, width) if spill else (16, width), BF16),
        pltpu.VMEM((2, 2 * half, width), BF16),
        pltpu.VMEM((groups * half, width), BF16),
        pltpu.VMEM((groups * half, width), BF16),
        pltpu.VMEM((2, micros, 2, rows, width), BF16),
        pltpu.VMEM((micros, rows, width), BF16),
        pltpu.VMEM((ffg, width), BF16),
        pltpu.VMEM((ffg, width), BF16),
        pltpu.VMEM((2, micros, 2, rows, width), BF16),
        pltpu.VMEM((2, micros, 2, rows, width), F32),
        pltpu.VMEM((2, micros, rows, width), BF16),
        pltpu.VMEM((2, micros, rows, width), BF16),
        pltpu.VMEM((2, micros, rows, width), BF16),
        pltpu.VMEM((micros, rows, width), BF16),
        pltpu.VMEM((2 * tiles, kept, ffg), F32),
        pltpu.VMEM((imgs, ffg), F32),
        pltpu.VMEM((2 * tiles, kept, width), F32),
        pltpu.VMEM((imgs, width), F32),
        pltpu.VMEM((4, imgs, width), F32),
        pltpu.VMEM((groups, imgs, width), F32),
        dma((2, 2 * nzp)), dma((2, groups)),
        dma((3, micros)), dma((2, micros, 2)),
        dma((2, micros)), dma((2, micros)),
        dma((micros,)), dma((micros,)),
        dma((micros,)), dma((micros,)),
        dma((4,)), dma((4,)),
        dma((n_pipe * groups,)), dma((groups,)),
        dma, dma((n_pipe,)),
        dma((nz,)), dma((nz,)),
        dma, dma,
        dma((n_pipe,)), dma,
        dma, dma,
        dma((2, 2 * nzp)), dma((2, groups)),
        dma((2,)), dma((2,)),
        dma((3, micros)), dma((2, micros, 2)),
        dma((2,)),
    ]
    if spill:
        outs = outs + [jax.ShapeDtypeStruct(eg_shape, BF16)]
        out_specs = out_specs + [pl.BlockSpec(memory_space=pl.ANY)]
    else:
        scratch = scratch + [pltpu.VMEM(eg_shape, BF16)]
    result = pl.pallas_call(
        functools.partial(kernel, cfg),
        out_shape=outs,
        in_specs=[sm, sm, vm, vm, vm, vm, vm, vm, vm],
        out_specs=out_specs,
        scratch_shapes=scratch,
        compiler_params=pltpu.CompilerParams(
            collective_id=0, has_side_effects=True, vmem_limit_bytes=60 * 2**20),
    )(scale, shift, ids, tids, vis.reshape(micros, rows, width), up[0].T, down[0], cap, prior)
    return result[0], result[1]


def solution(mesh):
    placed = (
        P(None, "dp", None, None),
        P("pipe", None, "dp"),
        P("pipe", "dp", None),
        P(("pipe", "dp"), None),
        P(("pipe", "dp"), None),
        P(),
        P(),
        P(),
    )
    return jax.shard_map(
        body,
        mesh=mesh,
        in_specs=placed,
        out_specs=(P(("pipe", "dp"), None), P(("pipe", "dp"), None)),
        check_vma=False,
    )
```

```python
import functools

import jax
import jax.numpy as jnp
from jax import lax
from jax.experimental import pallas as pl
from jax.experimental.pallas import tpu as pltpu
from jax.sharding import PartitionSpec as P

F32, BF16 = jnp.float32, jnp.bfloat16
SLOT = 32
MID = 16
TILE = 256
NT = (((1,), (1,)), ((), ()))
NN = (((1,), (0,)), ((), ()))


def dot(a, b, dims):
    return lax.dot_general(a, b, dims, preferred_element_type=F32)


def layer_norm(values):
    shifted = values - jnp.mean(values, axis=-1, keepdims=True)
    variance = jnp.mean(shifted * shifted, axis=-1, keepdims=True)
    return (shifted * lax.rsqrt(variance + 1e-06)).astype(BF16)


def unit_rows(values):
    total = jnp.sum(values * values, axis=-1, keepdims=True)
    return (values * lax.rsqrt(total + 1e-06)).astype(BF16)


def kernel(
    cfg,
    scale_ref, shift_ref, ids_ref, tids_ref, x_ref, up_ref, down_ref, cap_ref, prior_ref,
    img_ref, txt_ref, *rest,
):
    n_pipe, n_dp, micros, rows, width, ff, texts, priors, spill = cfg
    if spill:
        eg, *rest = rest
    else:
        *rest, eg = rest
    (own, chunk, w_ref, ul, dl, xl, rx, ug, dg, xg, part, sc, rc, sz, rz, ma, ma2, mx, mx2, tp, tall,
     mq, rq, pq, bq, mq_s, mq_r, pq_s, pq_r,
     w_s, w_r, x_s, x_r, c_s, c_r, z_s, z_r, h_s, h_r, tp_s, tp_r, ta_s, ta_r,
     ea_s, ea_r, ez_s, ez_r, ey_s, ey_r, ex_s, ex_r, ec_s, ec_r,
     hw_s, hw_r, hx_s, hx_r, xl_s, xl_r, loc) = rest
    p, d = lax.axis_index("pipe"), lax.axis_index("dp")
    c, y, z = d % 2, (d // 2) % 2, d // 4
    zb, zp = z % 2, z // 2
    nz = n_dp // 4
    nzp = nz // 2
    groups = 2 * nzp
    last = n_pipe - 1
    oc, oz = 1 - c, 1 - zb

    def at(z_, y_, c_):
        return (z_ * 2 + y_) * 2 + c_

    d_c, d_y, d_z = at(z, y, oc), at(z, 1 - y, c), at(zp * 2 + oz, y, c)

    def copy(src, dst, s, r, pipe, dp):
        return pltpu.make_async_remote_copy(
            src_ref=src, dst_ref=dst, send_sem=s, recv_sem=r,
            device_id=(pipe, dp), device_id_type=pl.DeviceIdType.MESH)

    def arrived(dst, r):
        copy(dst, dst, loc.at[0], r, p, d_c).wait_recv()

    def left(src, s):
        copy(src, src, s, loc.at[0], p, d_c).wait_send()

    barrier = pltpu.get_barrier_semaphore()
    total = n_pipe * n_dp

    def greet(i, _):
        t = (p * n_dp + d + i) % total
        pl.semaphore_signal(barrier, inc=1, device_id=(t // n_dp, t % n_dp),
                            device_id_type=pl.DeviceIdType.MESH)
        return 0

    lax.fori_loop(1, total, greet, 0)

    own[...] = jnp.zeros_like(own)
    own[0:texts, :] = unit_rows(cap_ref[...].astype(F32))
    own[MID:MID + priors, :] = unit_rows(prior_ref[...])

    @pl.when(p <= 1)
    def _():
        for m in range(micros):
            xl[zb, m, c] = x_ref[m]

    q = zp * 2 + y

    def wslot(ref, q_):
        return ref.at[pl.ds(pl.multiple_of(q_ * ff, 16), ff), :]

    shard = up_ref.shape[0]
    half = ul.shape[0] // groups
    for k, (ref, given) in enumerate(((ug, up_ref), (dg, down_ref))):
        w_ref[k, 0:shard, :] = given[...]
        if 2 * half > shard:
            w_ref[k, shard:2 * half, :] = jnp.zeros((2 * half - shard, width), BF16)
        ref[pl.ds(pl.multiple_of(q * ff, 16), ff), :] = w_ref[k, 0:ff, :]

    @pl.when(p == 0)
    def _():
        for k, ref in enumerate((ul, dl)):
            ref[pl.ds(pl.multiple_of(q * half, 16), half), :] = w_ref[k, 0:half, :]
    pl.semaphore_wait(barrier, total - 1)

    big = ((0, ug), (1, dg))

    def w_own_y(k, ref):
        return copy(w_ref.at[k, pl.ds(0, ff)], wslot(ref, q), w_s.at[k, 0], w_r.at[k, q], p, d_y)

    def w_own_z(k, ref, i):
        t = at(((zp + i) % nzp) * 2 + zb, y, c)
        return copy(w_ref.at[k, pl.ds(0, ff)], wslot(ref, q), w_s.at[k, i], w_r.at[k, q], p, t)

    def w_fwd(k, ref, i):
        q_ = ((zp + i) % nzp) * 2 + y
        return copy(wslot(ref, q_), wslot(ref, q_), w_s.at[k, nzp + i], w_r.at[k, q_], p, d_y)

    def x_c(buf, ss, rr, m):
        return copy(buf.at[zb, m, c], buf.at[zb, m, c], ss.at[0, m], rr.at[zb, m, c], p, d_c)

    def x_z(buf, ss, rr, m):
        return copy(buf.at[zb, m, c], buf.at[zb, m, c], ss.at[1, m], rr.at[zb, m, c], p, d_z)

    def x_f(buf, ss, rr, m):
        return copy(buf.at[oz, m, c], buf.at[oz, m, c], ss.at[2, m], rr.at[oz, m, c], p, d_c)

    def hslot(ref, q_):
        return ref.at[pl.ds(pl.multiple_of(q_ * half, 16), half), :]

    halves = ((0, ul), (1, dl))

    def h_over(k, ref):
        return copy(w_ref.at[k, pl.ds(half, half)], hslot(ref, q), hx_s.at[k], hx_r.at[k], 1, d)

    def h_start(k, ref):
        for i in range(1, nzp):
            t = at(((zp + i) % nzp) * 2 + zb, y, c)
            copy(hslot(ref, q), hslot(ref, q), hw_s.at[k, i], hw_r.at[k, q], p, t).start()
        copy(hslot(ref, q), hslot(ref, q), hw_s.at[k, 0], hw_r.at[k, q], p, d_y).start()

    def h_on(k, ref):
        for i in range(1, nzp):
            q_ = ((zp + i) % nzp) * 2 + y
            arrived(hslot(ref, q_), hw_r.at[k, q_])
            copy(hslot(ref, q_), hslot(ref, q_), hw_s.at[k, nzp + i], hw_r.at[k, q_], p, d_y).start()

    def h_here(k, ref):
        for i in range(nzp):
            q_ = ((zp + i) % nzp) * 2 + 1 - y
            arrived(hslot(ref, q_), hw_r.at[k, q_])

    def w_start(k, ref):
        for i in range(1, nzp):
            w_own_z(k, ref, i).start()
        w_own_y(k, ref).start()

    def w_on(k, ref):
        for i in range(1, nzp):
            q_ = ((zp + i) % nzp) * 2 + y
            arrived(wslot(ref, q_), w_r.at[k, q_])
            w_fwd(k, ref, i).start()

    def w_here(k, ref):
        for i in range(nzp):
            q_ = ((zp + i) % nzp) * 2 + 1 - y
            arrived(wslot(ref, q_), w_r.at[k, q_])

    def eslot(index, count):
        return eg.at[pl.ds(index, count)]

    e_own = ((c * 2 + y) * nz + z) * n_pipe + p
    e_z, e_y, e_c = ((c * 2 + y) * nz + z) * n_pipe, (c * 2 + y) * nz * n_pipe, c * 2 * nz * n_pipe
    many = 2 * nz * n_pipe
    send_a = copy(own, eg.at[e_own], ea_s, ea_r.at[p], last, d)
    send_y = copy(eslot(e_y, nz * n_pipe), eslot(e_y, nz * n_pipe), ey_s, ey_r, p, d_y)
    send_c = copy(eslot(e_c, many), eslot(e_c, many), ec_s, ec_r, p, d_c)

    def send_z(i):
        return copy(eslot(e_z, n_pipe), eslot(e_z, n_pipe), ez_s.at[i], ez_r.at[z], p,
                    at((z + i) % nz, y, c))

    def send_x(i):
        return copy(eslot(e_c, many), eslot(e_c, many), ex_s.at[i], ex_r, (p + i) % n_pipe, d)

    def tokens_out(buf, ss, rr, m):
        x_c(buf, ss, rr, m).start()
        x_z(buf, ss, rr, m).start()

    def tokens_on(buf, ss, rr):
        for m in range(micros):
            arrived(buf.at[oz, m, c], rr.at[oz, m, c])
            x_f(buf, ss, rr, m).start()

    def tokens_here(buf, rr):
        for m in range(micros):
            arrived(buf.at[zb, m, oc], rr.at[zb, m, oc])
            arrived(buf.at[oz, m, oc], rr.at[oz, m, oc])

    def emb_start():
        keep = pltpu.make_async_copy(own, eg.at[e_own], loc.at[1])
        keep.start()
        keep.wait()
        for t in range(last):
            arrived(eg.at[e_z + t], ea_r.at[t])
        for i in range(1, nz):
            send_z(i).start()

    def emb_middle():
        for i in range(1, nz):
            t = (z + i) % nz
            arrived(eslot(e_y + t * n_pipe, n_pipe), ez_r.at[t])
        send_y.start()

    def emb_end():
        arrived(eslot((c * 2 + 1 - y) * nz * n_pipe, nz * n_pipe), ey_r)
        send_c.start()
        for i in range(1, n_pipe):
            send_x(i).start()

    lx = (xl, xl_s, xl_r)
    gx = (xg, x_s, x_r)

    @pl.when(p != last)
    def _():
        send_a.start()

    @pl.when(p == 0)
    def _():
        h_over(0, ul).start()
        h_start(0, ul)
        h_over(1, dl).start()
        h_start(1, dl)
        for m in range(micros):
            tokens_out(*lx, m)
        h_on(0, ul)
        h_on(1, dl)

    @pl.when(p == 1)
    def _():
        for m in range(micros):
            tokens_out(*lx, m)
        arrived(hslot(ul, q), hx_r.at[0])
        h_start(0, ul)
        arrived(hslot(dl, q), hx_r.at[1])
        h_start(1, dl)
        h_on(0, ul)
        h_on(1, dl)

    @pl.when(p <= 1)
    def _():
        tokens_on(*lx)

    @pl.when(p > 0)
    def _():
        w_start(0, ug)

    @pl.when(p == last)
    def _():
        emb_start()

    if spill:
        ids_all, tids_all = ids_ref, tids_ref
    else:
        count = ids_ref.shape[1]
        square = (lax.broadcasted_iota(jnp.int32, (count, count), 0)
                  == lax.broadcasted_iota(jnp.int32, (count, count), 1))
        matches = jnp.max(jnp.where(square, ids_ref[...], -1), axis=1, keepdims=True)

        def look_up(index):
            shape = (count, index.shape[1])
            hit = lax.broadcasted_iota(jnp.int32, shape, 0) == index
            return jnp.max(jnp.where(hit, matches, -2), axis=0, keepdims=True)

        lane = lax.broadcasted_iota(jnp.int32, (1, total * SLOT), 1)
        s, r = lane // SLOT, lane % SLOT
        unit = s // n_pipe
        home = (s % n_pipe) * n_dp + ((unit % nz) * 2 + (unit // nz) % 2) * 2 + unit // (2 * nz)
        images = jnp.where((r >= MID) & (r < MID + priors), home * texts + 1 + r - MID, -1)
        ids_all = jnp.where(r < texts, home * texts + r, look_up(images))
        lane = lax.broadcasted_iota(jnp.int32, (1, 128), 1)
        m_, b_ = (lane // 2) % micros, (lane // (2 * micros)) % 2
        y_, z_ = (lane // (4 * micros)) % 2, lane // (8 * micros)
        home = m_ * n_dp + ((z_ * 2 + b_) * 2 + y_) * 2 + lane % 2
        tids_all = look_up(jnp.where(lane < tall.shape[0] * tall.shape[1], home * texts, -1))

    span = micros * 2 * rows
    tile = min(TILE, span)
    tiles = span // tile
    per = tile // rows
    mt = per // 2

    def activate(buf, u, b, j):
        values = buf[b, pl.ds(j * mt, mt)].reshape(tile, width).astype(F32)
        act = jax.nn.gelu(dot(layer_norm(values), u[...], NT), approximate=True)
        return values, act.astype(BF16)

    def to_core(b, m):
        return copy(sc.at[b, m], rc.at[b, m], c_s.at[b, m], c_r.at[b, m], p, d_c)

    def to_z(m):
        return copy(sz.at[0, m], rz.at[m], z_s.at[m], z_r.at[m], p, d_z)

    def reduce_rows(buf, u, dn, await_dn, between, emit):
        for first, b in ((True, oz), (False, zb)):
            def step(j, _, first=first, b=b):
                _, act = activate(buf, u, b, j)
                if first and tiles == 1:
                    await_dn()
                part[b, pl.ds(j * mt, mt)] = dot(act, dn[...], NN).reshape(mt, 2, rows, width)
                return 0

            if tiles == 1:
                step(0, 0)
            else:
                if first:
                    await_dn()
                lax.fori_loop(0, tiles, step, 0)
            for m in range(micros):
                sc[b, m] = part[b, m, oc].astype(BF16)
                to_core(b, m).start()
            if first:
                for m in range(micros):
                    arrived(rc.at[oz, m], c_r.at[oz, m])
                    sz[0, m] = (part[oz, m, c] + rc[oz, m].astype(F32)).astype(BF16)
                    to_z(m).start()
        between()
        for m in range(micros):
            arrived(rc.at[zb, m], c_r.at[zb, m])
            arrived(rz.at[m], z_r.at[m])
            emit(m, part[zb, m, c] + rc[zb, m].astype(F32) + rz[m].astype(F32))
        for m in range(micros):
            for b in range(2):
                left(sc.at[b, m], c_s.at[b, m])
            left(sz.at[0, m], z_s.at[m])

    def to_rx(m):
        return copy(sz.at[1, m], rx.at[m], h_s.at[m], h_r.at[m], 1, d)

    def hidden_out(m):
        return copy(sz.at[1, m], xg.at[zb, m, c], h_s.at[m], h_r.at[m],
                    jnp.minimum(p + 1, last), d)

    @pl.when(p <= 1)
    def _():
        h_here(0, ul)
        tokens_here(xl, xl_r)

        def await_dl():
            h_here(1, dl)

        def between():
            @pl.when(p == 1)
            def _():
                w_on(0, ug)
                if n_pipe > 2:
                    w_start(1, dg)

            @pl.when(p == last)
            def _():
                emb_middle()

        def emit(m, value):
            @pl.when(p == 0)
            def _():
                sz[1, m] = value.astype(BF16)
                to_rx(m).start()

            @pl.when(p == 1)
            def _():
                arrived(rx.at[m], h_r.at[m])
                new = value + rx[m].astype(F32) + xl[zb, m, c].astype(F32)
                xg[zb, m, c] = new.astype(BF16)
                tokens_out(*gx, m)

        reduce_rows(xl, ul, dl, await_dl, between, emit)

    def take_hidden():
        for m in range(micros):
            arrived(xg.at[zb, m, c], h_r.at[m])
            tokens_out(*gx, m)

    if n_pipe > 2:
        @pl.when(p > 1)
        def _():
            @pl.when(p < last)
            def _():
                w_start(1, dg)

            w_on(0, ug)

        @pl.when((p > 0) & (p < last))
        def _():
            @pl.when(p > 1)
            def _():
                take_hidden()

            tokens_on(*gx)
            w_on(1, dg)
            w_here(0, ug)
            tokens_here(xg, x_r)

            def emit(m, value):
                sz[1, m] = (value + xg[zb, m, c].astype(F32)).astype(BF16)
                hidden_out(m).start()

            reduce_rows(xg, ug, dg, lambda: w_here(1, dg), lambda: None, emit)

        @pl.when(p == last)
        def _():
            emb_middle()

    @pl.when(p == last)
    def _():
        emb_end()
        if n_pipe == 2:
            tokens_on(*gx)
        w_here(0, ug)
        arrived(eslot(oc * many, many), ec_r)

    @pl.when(p != last)
    def _():
        for m in range(micros):
            left(sz.at[1, m], h_s.at[m])
        arrived(eslot(e_c, many), ex_r)
        send_c.start()
        arrived(eslot(oc * many, many), ec_r)

    scale, shift = scale_ref[0], shift_ref[0]
    n_rows = total * SLOT
    cs = chunk.shape[0] if spill else n_rows
    ids_w = n_rows

    def column(ref, first, count, limit):
        lane = lax.broadcasted_iota(jnp.int32, (count, limit), 1)
        row = lax.broadcasted_iota(jnp.int32, (count, limit), 0)
        return jnp.max(jnp.where(lane == row + first, ref[...], -1), axis=1, keepdims=True)

    def weigh(scores, row_ids, col_ids, keep_mask):
        logits = scale * scores + shift
        positive = row_ids == col_ids
        w = jnp.where(positive, -scale * jax.nn.sigmoid(-logits), scale * jax.nn.sigmoid(logits))
        return jnp.where(keep_mask, w, 0.0).astype(BF16)

    def block(j):
        if not spill:
            return eg[...].reshape(n_rows, width), ids_all
        fetch = pltpu.make_async_copy(eg.at[pl.ds(j * (cs // SLOT), cs // SLOT)], chunk2, loc.at[1])
        fetch.start()
        fetch.wait()
        return chunk2[...].reshape(cs, width), ids_all[:, pl.ds(pl.multiple_of(j * cs, cs), cs)]

    chunk2 = chunk.reshape(cs // SLOT, SLOT, width) if spill else None
    own_v = own[...]
    own_ids = column(ids_all, e_own * SLOT, SLOT, ids_w)
    kind_r = lax.broadcasted_iota(jnp.int32, (SLOT, cs), 0)
    kind_c = lax.broadcasted_iota(jnp.int32, (SLOT, cs), 1) % SLOT
    text_c = kind_c < texts
    prior_c = (kind_c >= MID) & (kind_c < MID + priors)
    mask = ((kind_r < texts) & prior_c) | ((kind_r >= MID) & text_c)

    def early(j, acc):
        e, ids = block(j)
        w = weigh(dot(own_v, e, NT), own_ids, ids, mask)
        return acc + dot(w, e, NN)

    if spill:
        grads = lax.fori_loop(0, n_rows // cs, early, jnp.zeros((SLOT, width), F32))
    else:
        grads = early(0, 0.0)
    img_ref[1:1 + priors, :] = grads[MID:MID + priors]

    @pl.when(p == last)
    def _():
        def step(i, _):
            b, j = i // tiles, i % tiles
            values, act = activate(xg, ug, b, j)
            ma[i] = jnp.mean(act.astype(F32).reshape(per, rows, -1), axis=1)
            mx[i] = jnp.mean(values.reshape(per, rows, width), axis=1)
            return 0

        if n_pipe > 2:
            take_hidden()
            tokens_on(*gx)
        tokens_here(xg, x_r)
        lax.fori_loop(0, 2 * tiles, step, 0)
        for i in range(2 * tiles):
            ma2[i * per:(i + 1) * per, :] = ma[i]
            mx2[i * per:(i + 1) * per, :] = mx[i]
        t = zb * 2 + c
        for g in range(groups):
            mq[g] = ma2[:, g * ff:(g + 1) * ff]
        rq[q] = mq[q]

        def across(src, dst, ss, rr, i):
            g = (q + i) % groups
            return copy(src.at[g], dst.at[q], ss.at[i], rr.at[q], p,
                        at((g // 2) * 2 + zb, g % 2, c))

        for i in range(1, groups):
            across(mq, rq, mq_s, mq_r, i).start()
        for i in range(1, groups):
            g = (q + i) % groups
            arrived(rq.at[g], mq_r.at[g])
        means = rq[...].reshape(groups * rq.shape[1], ff).astype(BF16)
        pq[...] = dot(means, w_ref[1, 0:ff, :], NN).reshape(pq.shape)
        bq[q] = pq[q]
        for i in range(1, groups):
            across(pq, bq, pq_s, pq_r, i).start()
        for i in range(1, groups):
            g = (q + i) % groups
            arrived(bq.at[g], pq_r.at[g])
        tp[t] = jnp.sum(bq[...], axis=0)
        for i in range(1, groups):
            left(mq.at[q], mq_s.at[i])
            left(pq.at[q], pq_s.at[i])

        def t_out(i):
            t_ = (t + i) % 4
            return copy(tp.at[t], tp.at[t], tp_s.at[i], tp_r.at[t], p,
                        at(zp * 2 + t_ // 2, y, t_ % 2))

        for i in range(1, 4):
            t_out(i).start()
        for i in range(1, 4):
            t_ = (t + i) % 4
            arrived(tp.at[t_], tp_r.at[t_])
        pooled = mx2[...] + (tp[0] + tp[1]) + (tp[2] + tp[3])
        tall[q] = unit_rows(pooled).astype(F32)

        def spread(i, _):
            s = (last * groups + q + i) % (n_pipe * groups)
            g = s % groups
            copy(tall.at[q], tall.at[q], ta_s.at[i], ta_r.at[q], s // groups,
                 at((g // 2) * 2 + zb, g % 2, c)).start()
            return 0

        lax.fori_loop(1, n_pipe * groups, spread, 0)
        for i in range(1, 4):
            left(tp.at[t], tp_s.at[i])
        for i in range(1, groups):
            g = (q + i) % groups
            arrived(tall.at[g], ta_r.at[g])
        for i in range(1, n_pipe * groups):
            left(tall.at[q], ta_s.at[i])

    @pl.when(p != last)
    def _():
        for g in range(groups):
            arrived(tall.at[g], ta_r.at[g])

    n_t = tall.shape[0] * tall.shape[1]
    towers = tall[...].reshape(n_t, width).astype(BF16)
    t_ids = tids_all[...][:, :n_t]
    rmask = lax.broadcasted_iota(jnp.int32, (SLOT, n_t), 0) < texts
    w = weigh(dot(own_v, towers, NT), own_ids, t_ids, rmask)
    txt_ref[...] = (grads + dot(w, towers, NN))[:texts]

    mine = (zb * micros + p) * 2 + c
    pick = lax.broadcasted_iota(jnp.int32, (tall.shape[1], width), 0) == mine
    row = jnp.sum(jnp.where(pick, tall[q], 0.0), axis=0, keepdims=True)
    row8 = jnp.broadcast_to(row, (8, width)).astype(BF16)
    row_id = column(tids_all, q * tall.shape[1] + mine, 1, tids_all.shape[1])
    row_ids = jnp.broadcast_to(row_id, (8, 1))

    def late(j, acc):
        e, ids = block(j)
        w = weigh(dot(row8, e, NT), row_ids, ids, text_c[:8])
        return acc + dot(w, e, NN)

    if spill:
        g_row = lax.fori_loop(0, n_rows // cs, late, jnp.zeros((8, width), F32))
    else:
        g_row = late(0, 0.0)
    img_ref[0:1, :] = g_row[0:1]

    @pl.when(p > 0)
    def _():
        def gone(k):
            for i in range(nzp):
                left(w_ref.at[k, pl.ds(0, ff)], w_s.at[k, i])
            for i in range(1, nzp):
                left(w_ref.at[k, pl.ds(0, ff)], w_s.at[k, nzp + i])

        gone(0)
        if n_pipe > 2:
            pl.when(p < last)(lambda: gone(1))
        for m in range(micros):
            for i in range(3):
                left(xg.at[zb, m, c], x_s.at[i, m])

    @pl.when(p == 0)
    def _():
        for k in range(2):
            left(w_ref.at[k, pl.ds(half, half)], hx_s.at[k])

    @pl.when(p <= 1)
    def _():
        for k, ref in halves:
            for i in range(nzp):
                left(hslot(ref, q), hw_s.at[k, i])
            for i in range(1, nzp):
                left(hslot(ref, q), hw_s.at[k, nzp + i])
        for m in range(micros):
            for i in range(3):
                left(xl.at[zb, m, c], xl_s.at[i, m])

    send_c.wait_send()

    @pl.when(p == last)
    def _():
        for i in range(1, nz):
            left(eslot(e_z, n_pipe), ez_s.at[i])
        send_y.wait_send()
        for i in range(1, n_pipe):
            left(eslot(e_c, many), ex_s.at[i])

    @pl.when(p != last)
    def _():
        send_a.wait_send()


def id_rows(match, n_pipe, nz, texts, priors):
    total = n_pipe * nz * 4

    def placed(numbers):
        numbers = numbers.reshape(n_pipe, nz, 2, 2, texts)
        return numbers.transpose(3, 2, 1, 0, 4).reshape(total, texts)

    ids = jnp.concatenate([
        jnp.pad(placed(jnp.arange(total * texts, dtype=jnp.int32)),
                ((0, 0), (0, MID - texts)), constant_values=-2),
        jnp.pad(placed(match)[:, 1:], ((0, 0), (0, SLOT - MID - priors)), constant_values=-2),
    ], axis=1).reshape(1, total * SLOT)
    tids = match.reshape(n_pipe, nz // 2, 2, 2, 2, texts)[..., 0]
    tids = tids.transpose(1, 3, 2, 0, 4).reshape(1, -1)
    tids = jnp.pad(tids, ((0, 0), (0, -tids.shape[1] % 128)), constant_values=-2)
    return ids, tids


def body(vis, up, down, cap, prior, match, scale, shift):
    n_pipe, n_dp = lax.axis_size("pipe"), lax.axis_size("dp")
    micros, img_mb, patch, width = vis.shape
    rows = img_mb * patch
    shard = up.shape[2]
    ff = -(-shard // 16) * 16
    texts, priors = cap.shape[0], prior.shape[0]
    nz, total = n_dp // 4, n_pipe * n_dp
    nzp = nz // 2
    groups = 2 * nzp
    spill = total > 64
    if spill:
        ids, tids = id_rows(match, n_pipe, nz, texts, priors)
    else:
        ids = tids = match.reshape(1, -1)
    cfg = (n_pipe, n_dp, micros, rows, width, ff, texts, priors, spill)
    span = micros * 2 * rows
    tile = min(TILE, span)
    tiles, kept = span // tile, tile // rows
    imgs = 4 * micros
    ffg = groups * ff
    half = -(-ff // 32) * 16
    vm = pl.BlockSpec(memory_space=pltpu.VMEM)
    sm = pl.BlockSpec(memory_space=pltpu.SMEM)
    dma = pltpu.SemaphoreType.DMA
    outs = [jax.ShapeDtypeStruct((texts, width), F32)] * 2
    out_specs = [vm, vm]
    eg_shape = (total, SLOT, width)
    scratch = [
        pltpu.VMEM((SLOT, width), BF16),
        pltpu.VMEM((1024, width) if spill else (16, width), BF16),
        pltpu.VMEM((2, 2 * half, width), BF16),
        pltpu.VMEM((groups * half, width), BF16),
        pltpu.VMEM((groups * half, width), BF16),
        pltpu.VMEM((2, micros, 2, rows, width), BF16),
        pltpu.VMEM((micros, rows, width), BF16),
        pltpu.VMEM((ffg, width), BF16),
        pltpu.VMEM((ffg, width), BF16),
        pltpu.VMEM((2, micros, 2, rows, width), BF16),
        pltpu.VMEM((2, micros, 2, rows, width), F32),
        pltpu.VMEM((2, micros, rows, width), BF16),
        pltpu.VMEM((2, micros, rows, width), BF16),
        pltpu.VMEM((2, micros, rows, width), BF16),
        pltpu.VMEM((micros, rows, width), BF16),
        pltpu.VMEM((2 * tiles, kept, ffg), F32),
        pltpu.VMEM((imgs, ffg), F32),
        pltpu.VMEM((2 * tiles, kept, width), F32),
        pltpu.VMEM((imgs, width), F32),
        pltpu.VMEM((4, imgs, width), F32),
        pltpu.VMEM((groups, imgs, width), F32),
        pltpu.VMEM((groups, imgs, ff), F32),
        pltpu.VMEM((groups, imgs, ff), F32),
        pltpu.VMEM((groups, imgs, width), F32),
        pltpu.VMEM((groups, imgs, width), F32),
        dma((groups,)), dma((groups,)), dma((groups,)), dma((groups,)),
        dma((2, 2 * nzp)), dma((2, groups)),
        dma((3, micros)), dma((2, micros, 2)),
        dma((2, micros)), dma((2, micros)),
        dma((micros,)), dma((micros,)),
        dma((micros,)), dma((micros,)),
        dma((4,)), dma((4,)),
        dma((n_pipe * groups,)), dma((groups,)),
        dma, dma((n_pipe,)),
        dma((nz,)), dma((nz,)),
        dma, dma,
        dma((n_pipe,)), dma,
        dma, dma,
        dma((2, 2 * nzp)), dma((2, groups)),
        dma((2,)), dma((2,)),
        dma((3, micros)), dma((2, micros, 2)),
        dma((2,)),
    ]
    if spill:
        outs = outs + [jax.ShapeDtypeStruct(eg_shape, BF16)]
        out_specs = out_specs + [pl.BlockSpec(memory_space=pl.ANY)]
    else:
        scratch = scratch + [pltpu.VMEM(eg_shape, BF16)]
    result = pl.pallas_call(
        functools.partial(kernel, cfg),
        out_shape=outs,
        in_specs=[sm, sm, vm, vm, vm, vm, vm, vm, vm],
        out_specs=out_specs,
        scratch_shapes=scratch,
        compiler_params=pltpu.CompilerParams(
            collective_id=0, has_side_effects=True, vmem_limit_bytes=60 * 2**20),
    )(scale, shift, ids, tids, vis.reshape(micros, rows, width), up[0].T, down[0], cap, prior)
    return result[0], result[1]


def solution(mesh):
    placed = (
        P(None, "dp", None, None),
        P("pipe", None, "dp"),
        P("pipe", "dp", None),
        P(("pipe", "dp"), None),
        P(("pipe", "dp"), None),
        P(),
        P(),
        P(),
    )
    return jax.shard_map(
        body,
        mesh=mesh,
        in_specs=placed,
        out_specs=(P(("pipe", "dp"), None), P(("pipe", "dp"), None)),
        check_vma=False,
    )
```

```python
import functools

import jax
import jax.numpy as jnp
from jax import lax
from jax.experimental import pallas as pl
from jax.experimental.pallas import tpu as pltpu
from jax.sharding import PartitionSpec as P

F32, BF16 = jnp.float32, jnp.bfloat16
SLOT = 32
MID = 16
TILE = 256
NT = (((1,), (1,)), ((), ()))
NN = (((1,), (0,)), ((), ()))


def dot(a, b, dims):
    return lax.dot_general(a, b, dims, preferred_element_type=F32)


def layer_norm(values):
    shifted = values - jnp.mean(values, axis=-1, keepdims=True)
    variance = jnp.mean(shifted * shifted, axis=-1, keepdims=True)
    return (shifted * lax.rsqrt(variance + 1e-06)).astype(BF16)


def unit_rows(values):
    total = jnp.sum(values * values, axis=-1, keepdims=True)
    return (values * lax.rsqrt(total + 1e-06)).astype(BF16)


def kernel(
    cfg,
    scale_ref, shift_ref, ids_ref, tids_ref, x_ref, up_ref, down_ref, cap_ref, prior_ref,
    img_ref, txt_ref, *rest,
):
    n_pipe, n_dp, micros, rows, width, ff, texts, priors, spill = cfg
    if spill:
        eg, *rest = rest
    else:
        *rest, eg = rest
    (own, chunk, w_ref, ug, dg, xg, part, sc, rc, sz, rz, ma, ma2, mx, mx2, tp, tall,
     mq, rq, pq, bq, mq_s, mq_r, pq_s, pq_r,
     w_s, w_r, x_s, x_r, c_s, c_r, z_s, z_r, h_s, h_r, tp_s, tp_r, ta_s, ta_r,
     ea_s, ea_r, ez_s, ez_r, ey_s, ey_r, ex_s, ex_r, ec_s, ec_r, loc) = rest
    p, d = lax.axis_index("pipe"), lax.axis_index("dp")
    c, y, z = d % 2, (d // 2) % 2, d // 4
    zb, zp = z % 2, z // 2
    nz = n_dp // 4
    nzp = nz // 2
    groups = 2 * nzp
    last = n_pipe - 1
    oc, oz = 1 - c, 1 - zb

    def at(z_, y_, c_):
        return (z_ * 2 + y_) * 2 + c_

    d_c, d_y, d_z = at(z, y, oc), at(z, 1 - y, c), at(zp * 2 + oz, y, c)

    def copy(src, dst, s, r, pipe, dp):
        return pltpu.make_async_remote_copy(
            src_ref=src, dst_ref=dst, send_sem=s, recv_sem=r,
            device_id=(pipe, dp), device_id_type=pl.DeviceIdType.MESH)

    def arrived(dst, r):
        copy(dst, dst, loc.at[0], r, p, d_c).wait_recv()

    def left(src, s):
        copy(src, src, s, loc.at[0], p, d_c).wait_send()

    barrier = pltpu.get_barrier_semaphore()
    total = n_pipe * n_dp

    def greet(i, _):
        t = (p * n_dp + d + i) % total
        pl.semaphore_signal(barrier, inc=1, device_id=(t // n_dp, t % n_dp),
                            device_id_type=pl.DeviceIdType.MESH)
        return 0

    lax.fori_loop(1, total, greet, 0)

    own[...] = jnp.zeros_like(own)
    own[0:texts, :] = unit_rows(cap_ref[...].astype(F32))
    own[MID:MID + priors, :] = unit_rows(prior_ref[...])

    @pl.when(p == 0)
    def _():
        for m in range(micros):
            xg[zb, m, c] = x_ref[m]

    q = zp * 2 + y

    def wslot(ref, q_):
        return ref.at[pl.ds(pl.multiple_of(q_ * ff, 16), ff), :]

    shard = up_ref.shape[0]
    for k, (ref, given) in enumerate(((ug, up_ref), (dg, down_ref))):
        w_ref[k, 0:shard, :] = given[...]
        if ff > shard:
            w_ref[k, shard:ff, :] = jnp.zeros((ff - shard, width), BF16)
        ref[pl.ds(pl.multiple_of(q * ff, 16), ff), :] = w_ref[k]
    pl.semaphore_wait(barrier, total - 1)

    big = ((0, ug), (1, dg))

    def w_own_y(k, ref):
        return copy(w_ref.at[k], wslot(ref, q), w_s.at[k, 0], w_r.at[k, q], p, d_y)

    def w_own_z(k, ref, i):
        t = at(((zp + i) % nzp) * 2 + zb, y, c)
        return copy(w_ref.at[k], wslot(ref, q), w_s.at[k, i], w_r.at[k, q], p, t)

    def w_fwd(k, ref, i):
        q_ = ((zp + i) % nzp) * 2 + y
        return copy(wslot(ref, q_), wslot(ref, q_), w_s.at[k, nzp + i], w_r.at[k, q_], p, d_y)

    def x_c(m):
        return copy(xg.at[zb, m, c], xg.at[zb, m, c], x_s.at[0, m], x_r.at[zb, m, c], p, d_c)

    def x_z(m):
        return copy(xg.at[zb, m, c], xg.at[zb, m, c], x_s.at[1, m], x_r.at[zb, m, c], p, d_z)

    def x_f(m):
        return copy(xg.at[oz, m, c], xg.at[oz, m, c], x_s.at[2, m], x_r.at[oz, m, c], p, d_c)

    def w_start(k, ref):
        for i in range(1, nzp):
            w_own_z(k, ref, i).start()
        w_own_y(k, ref).start()

    def w_on(k, ref):
        for i in range(1, nzp):
            q_ = ((zp + i) % nzp) * 2 + y
            arrived(wslot(ref, q_), w_r.at[k, q_])
            w_fwd(k, ref, i).start()

    def w_here(k, ref):
        for i in range(nzp):
            q_ = ((zp + i) % nzp) * 2 + 1 - y
            arrived(wslot(ref, q_), w_r.at[k, q_])

    def eslot(index, count):
        return eg.at[pl.ds(index, count)]

    e_own = ((c * 2 + y) * nz + z) * n_pipe + p
    e_z, e_y, e_c = ((c * 2 + y) * nz + z) * n_pipe, (c * 2 + y) * nz * n_pipe, c * 2 * nz * n_pipe
    many = 2 * nz * n_pipe
    send_a = copy(own, eg.at[e_own], ea_s, ea_r.at[p], last, d)
    send_y = copy(eslot(e_y, nz * n_pipe), eslot(e_y, nz * n_pipe), ey_s, ey_r, p, d_y)
    send_c = copy(eslot(e_c, many), eslot(e_c, many), ec_s, ec_r, p, d_c)

    def send_z(i):
        return copy(eslot(e_z, n_pipe), eslot(e_z, n_pipe), ez_s.at[i], ez_r.at[z], p,
                    at((z + i) % nz, y, c))

    def send_x(i):
        return copy(eslot(e_c, many), eslot(e_c, many), ex_s.at[i], ex_r, (p + i) % n_pipe, d)

    def tokens_on():
        for m in range(micros):
            arrived(xg.at[oz, m, c], x_r.at[oz, m, c])
            x_f(m).start()

    def tokens_here():
        for m in range(micros):
            arrived(xg.at[zb, m, oc], x_r.at[zb, m, oc])
            arrived(xg.at[oz, m, oc], x_r.at[oz, m, oc])

    w_start(0, ug)

    @pl.when(p == 0)
    def _():
        for m in range(micros):
            x_c(m).start()
            x_z(m).start()

    @pl.when(p != last)
    def _():
        send_a.start()
        w_start(1, dg)
        w_on(0, ug)

    @pl.when(p == 0)
    def _():
        tokens_on()

    @pl.when(p == last)
    def _():
        keep = pltpu.make_async_copy(own, eg.at[e_own], loc.at[1])
        keep.start()
        keep.wait()
        for t in range(last):
            arrived(eg.at[e_z + t], ea_r.at[t])
        for i in range(1, nz):
            send_z(i).start()
        w_on(0, ug)
        for i in range(1, nz):
            t = (z + i) % nz
            arrived(eslot(e_y + t * n_pipe, n_pipe), ez_r.at[t])
        send_y.start()
        arrived(eslot((c * 2 + 1 - y) * nz * n_pipe, nz * n_pipe), ey_r)
        send_c.start()
        for i in range(1, n_pipe):
            send_x(i).start()
        w_here(0, ug)
        arrived(eslot(oc * many, many), ec_r)

    @pl.when(p != last)
    def _():
        w_on(1, dg)
        w_here(0, ug)

    if spill:
        ids_all, tids_all = ids_ref, tids_ref
    else:
        count = ids_ref.shape[1]
        square = (lax.broadcasted_iota(jnp.int32, (count, count), 0)
                  == lax.broadcasted_iota(jnp.int32, (count, count), 1))
        matches = jnp.max(jnp.where(square, ids_ref[...], -1), axis=1, keepdims=True)

        def look_up(index):
            shape = (count, index.shape[1])
            hit = lax.broadcasted_iota(jnp.int32, shape, 0) == index
            return jnp.max(jnp.where(hit, matches, -2), axis=0, keepdims=True)

        lane = lax.broadcasted_iota(jnp.int32, (1, total * SLOT), 1)
        s, r = lane // SLOT, lane % SLOT
        unit = s // n_pipe
        home = (s % n_pipe) * n_dp + ((unit % nz) * 2 + (unit // nz) % 2) * 2 + unit // (2 * nz)
        images = jnp.where((r >= MID) & (r < MID + priors), home * texts + 1 + r - MID, -1)
        ids_all = jnp.where(r < texts, home * texts + r, look_up(images))
        lane = lax.broadcasted_iota(jnp.int32, (1, 128), 1)
        m_, b_ = (lane // 2) % micros, (lane // (2 * micros)) % 2
        y_, z_ = (lane // (4 * micros)) % 2, lane // (8 * micros)
        home = m_ * n_dp + ((z_ * 2 + b_) * 2 + y_) * 2 + lane % 2
        tids_all = look_up(jnp.where(lane < tall.shape[0] * tall.shape[1], home * texts, -1))

    span = micros * 2 * rows
    tile = min(TILE, span)
    tiles = span // tile
    per = tile // rows
    mt = per // 2

    def activate(b, j):
        values = xg[b, pl.ds(j * mt, mt)].reshape(tile, width).astype(F32)
        act = jax.nn.gelu(dot(layer_norm(values), ug[...], NT), approximate=True)
        return values, act.astype(BF16)

    def hidden_out(m):
        return copy(sz.at[1, m], xg.at[zb, m, c], h_s.at[m], h_r.at[m],
                    jnp.minimum(p + 1, last), d)

    def to_core(b, m):
        return copy(sc.at[b, m], rc.at[b, m], c_s.at[b, m], c_r.at[b, m], p, d_c)

    def to_z(m):
        return copy(sz.at[0, m], rz.at[m], z_s.at[m], z_r.at[m], p, d_z)

    def take_hidden():
        for m in range(micros):
            arrived(xg.at[zb, m, c], h_r.at[m])
            x_c(m).start()
            x_z(m).start()
        tokens_on()

    @pl.when((p > 0) & (p < last))
    def _():
        take_hidden()

    @pl.when(p < last)
    def _():
        tokens_here()
        if tiles > 1:
            w_here(1, dg)
        for b in (oz, zb):
            def step(j, _, b=b):
                _, act = activate(b, j)
                if b is oz and tiles == 1:
                    w_here(1, dg)
                out = dot(act, dg[...], NN)
                part[b, pl.ds(j * mt, mt)] = out.reshape(mt, 2, rows, width)
                return 0

            if tiles == 1:
                step(0, 0)
            else:
                lax.fori_loop(0, tiles, step, 0)
            for m in range(micros):
                sc[b, m] = part[b, m, oc].astype(BF16)
                to_core(b, m).start()
            if b is oz:
                for m in range(micros):
                    arrived(rc.at[oz, m], c_r.at[oz, m])
                    sz[0, m] = (part[oz, m, c] + rc[oz, m].astype(F32)).astype(BF16)
                    to_z(m).start()
        for m in range(micros):
            arrived(rc.at[zb, m], c_r.at[zb, m])
            arrived(rz.at[m], z_r.at[m])
            new = part[zb, m, c] + rc[zb, m].astype(F32) + rz[m].astype(F32)
            sz[1, m] = (new + xg[zb, m, c].astype(F32)).astype(BF16)
            hidden_out(m).start()
        for m in range(micros):
            for b in range(2):
                left(sc.at[b, m], c_s.at[b, m])
            left(sz.at[0, m], z_s.at[m])
            left(sz.at[1, m], h_s.at[m])

        arrived(eslot(e_c, many), ex_r)
        send_c.start()
        arrived(eslot(oc * many, many), ec_r)

    scale, shift = scale_ref[0], shift_ref[0]
    n_rows = total * SLOT
    cs = chunk.shape[0] if spill else n_rows
    ids_w = n_rows

    def column(ref, first, count, limit):
        lane = lax.broadcasted_iota(jnp.int32, (count, limit), 1)
        row = lax.broadcasted_iota(jnp.int32, (count, limit), 0)
        return jnp.max(jnp.where(lane == row + first, ref[...], -1), axis=1, keepdims=True)

    def weigh(scores, row_ids, col_ids, keep_mask):
        logits = scale * scores + shift
        positive = row_ids == col_ids
        w = jnp.where(positive, -scale * jax.nn.sigmoid(-logits), scale * jax.nn.sigmoid(logits))
        return jnp.where(keep_mask, w, 0.0).astype(BF16)

    def block(j):
        if not spill:
            return eg[...].reshape(n_rows, width), ids_all
        fetch = pltpu.make_async_copy(eg.at[pl.ds(j * (cs // SLOT), cs // SLOT)], chunk2, loc.at[1])
        fetch.start()
        fetch.wait()
        return chunk2[...].reshape(cs, width), ids_all[:, pl.ds(pl.multiple_of(j * cs, cs), cs)]

    chunk2 = chunk.reshape(cs // SLOT, SLOT, width) if spill else None
    own_v = own[...]
    own_ids = column(ids_all, e_own * SLOT, SLOT, ids_w)
    kind_r = lax.broadcasted_iota(jnp.int32, (SLOT, cs), 0)
    kind_c = lax.broadcasted_iota(jnp.int32, (SLOT, cs), 1) % SLOT
    text_c = kind_c < texts
    prior_c = (kind_c >= MID) & (kind_c < MID + priors)
    mask = ((kind_r < texts) & prior_c) | ((kind_r >= MID) & text_c)

    def early(j, acc):
        e, ids = block(j)
        w = weigh(dot(own_v, e, NT), own_ids, ids, mask)
        return acc + dot(w, e, NN)

    if spill:
        grads = lax.fori_loop(0, n_rows // cs, early, jnp.zeros((SLOT, width), F32))
    else:
        grads = early(0, 0.0)
    img_ref[1:1 + priors, :] = grads[MID:MID + priors]

    @pl.when(p == last)
    def _():
        def step(i, _):
            b, j = i // tiles, i % tiles
            values, act = activate(b, j)
            ma[i] = jnp.mean(act.astype(F32).reshape(per, rows, -1), axis=1)
            mx[i] = jnp.mean(values.reshape(per, rows, width), axis=1)
            return 0

        take_hidden()
        tokens_here()
        lax.fori_loop(0, 2 * tiles, step, 0)
        for i in range(2 * tiles):
            ma2[i * per:(i + 1) * per, :] = ma[i]
            mx2[i * per:(i + 1) * per, :] = mx[i]
        t = zb * 2 + c
        for g in range(groups):
            mq[g] = ma2[:, g * ff:(g + 1) * ff]
        rq[q] = mq[q]

        def across(src, dst, ss, rr, i):
            g = (q + i) % groups
            return copy(src.at[g], dst.at[q], ss.at[i], rr.at[q], p,
                        at((g // 2) * 2 + zb, g % 2, c))

        for i in range(1, groups):
            across(mq, rq, mq_s, mq_r, i).start()
        for i in range(1, groups):
            g = (q + i) % groups
            arrived(rq.at[g], mq_r.at[g])
        means = rq[...].reshape(groups * rq.shape[1], ff).astype(BF16)
        pq[...] = dot(means, w_ref[1, 0:ff, :], NN).reshape(pq.shape)
        bq[q] = pq[q]
        for i in range(1, groups):
            across(pq, bq, pq_s, pq_r, i).start()
        for i in range(1, groups):
            g = (q + i) % groups
            arrived(bq.at[g], pq_r.at[g])
        tp[t] = jnp.sum(bq[...], axis=0)
        for i in range(1, groups):
            left(mq.at[q], mq_s.at[i])
            left(pq.at[q], pq_s.at[i])

        def t_out(i):
            t_ = (t + i) % 4
            return copy(tp.at[t], tp.at[t], tp_s.at[i], tp_r.at[t], p,
                        at(zp * 2 + t_ // 2, y, t_ % 2))

        for i in range(1, 4):
            t_out(i).start()
        for i in range(1, 4):
            t_ = (t + i) % 4
            arrived(tp.at[t_], tp_r.at[t_])
        pooled = mx2[...] + (tp[0] + tp[1]) + (tp[2] + tp[3])
        tall[q] = unit_rows(pooled).astype(F32)

        def spread(i, _):
            s = (last * groups + q + i) % (n_pipe * groups)
            g = s % groups
            copy(tall.at[q], tall.at[q], ta_s.at[i], ta_r.at[q], s // groups,
                 at((g // 2) * 2 + zb, g % 2, c)).start()
            return 0

        lax.fori_loop(1, n_pipe * groups, spread, 0)
        for i in range(1, 4):
            left(tp.at[t], tp_s.at[i])
        for i in range(1, groups):
            g = (q + i) % groups
            arrived(tall.at[g], ta_r.at[g])
        for i in range(1, n_pipe * groups):
            left(tall.at[q], ta_s.at[i])

    @pl.when(p != last)
    def _():
        for g in range(groups):
            arrived(tall.at[g], ta_r.at[g])

    n_t = tall.shape[0] * tall.shape[1]
    towers = tall[...].reshape(n_t, width).astype(BF16)
    t_ids = tids_all[...][:, :n_t]
    rmask = lax.broadcasted_iota(jnp.int32, (SLOT, n_t), 0) < texts
    w = weigh(dot(own_v, towers, NT), own_ids, t_ids, rmask)
    txt_ref[...] = (grads + dot(w, towers, NN))[:texts]

    mine = (zb * micros + p) * 2 + c
    pick = lax.broadcasted_iota(jnp.int32, (tall.shape[1], width), 0) == mine
    row = jnp.sum(jnp.where(pick, tall[q], 0.0), axis=0, keepdims=True)
    row8 = jnp.broadcast_to(row, (8, width)).astype(BF16)
    row_id = column(tids_all, q * tall.shape[1] + mine, 1, tids_all.shape[1])
    row_ids = jnp.broadcast_to(row_id, (8, 1))

    def late(j, acc):
        e, ids = block(j)
        w = weigh(dot(row8, e, NT), row_ids, ids, text_c[:8])
        return acc + dot(w, e, NN)

    if spill:
        g_row = lax.fori_loop(0, n_rows // cs, late, jnp.zeros((8, width), F32))
    else:
        g_row = late(0, 0.0)
    img_ref[0:1, :] = g_row[0:1]

    def gone(k):
        for i in range(nzp):
            left(w_ref.at[k], w_s.at[k, i])
        for i in range(1, nzp):
            left(w_ref.at[k], w_s.at[k, nzp + i])

    gone(0)
    pl.when(p < last)(lambda: gone(1))
    for m in range(micros):
        for i in range(3):
            left(xg.at[zb, m, c], x_s.at[i, m])
    send_c.wait_send()

    @pl.when(p == last)
    def _():
        for i in range(1, nz):
            left(eslot(e_z, n_pipe), ez_s.at[i])
        send_y.wait_send()
        for i in range(1, n_pipe):
            left(eslot(e_c, many), ex_s.at[i])

    @pl.when(p != last)
    def _():
        send_a.wait_send()


def id_rows(match, n_pipe, nz, texts, priors):
    total = n_pipe * nz * 4

    def placed(numbers):
        numbers = numbers.reshape(n_pipe, nz, 2, 2, texts)
        return numbers.transpose(3, 2, 1, 0, 4).reshape(total, texts)

    ids = jnp.concatenate([
        jnp.pad(placed(jnp.arange(total * texts, dtype=jnp.int32)),
                ((0, 0), (0, MID - texts)), constant_values=-2),
        jnp.pad(placed(match)[:, 1:], ((0, 0), (0, SLOT - MID - priors)), constant_values=-2),
    ], axis=1).reshape(1, total * SLOT)
    tids = match.reshape(n_pipe, nz // 2, 2, 2, 2, texts)[..., 0]
    tids = tids.transpose(1, 3, 2, 0, 4).reshape(1, -1)
    tids = jnp.pad(tids, ((0, 0), (0, -tids.shape[1] % 128)), constant_values=-2)
    return ids, tids


def body(vis, up, down, cap, prior, match, scale, shift):
    n_pipe, n_dp = lax.axis_size("pipe"), lax.axis_size("dp")
    micros, img_mb, patch, width = vis.shape
    rows = img_mb * patch
    shard = up.shape[2]
    ff = -(-shard // 16) * 16
    texts, priors = cap.shape[0], prior.shape[0]
    nz, total = n_dp // 4, n_pipe * n_dp
    nzp = nz // 2
    groups = 2 * nzp
    spill = total > 64
    if spill:
        ids, tids = id_rows(match, n_pipe, nz, texts, priors)
    else:
        ids = tids = match.reshape(1, -1)
    cfg = (n_pipe, n_dp, micros, rows, width, ff, texts, priors, spill)
    span = micros * 2 * rows
    tile = min(TILE, span)
    tiles, kept = span // tile, tile // rows
    imgs = 4 * micros
    ffg = groups * ff
    vm = pl.BlockSpec(memory_space=pltpu.VMEM)
    sm = pl.BlockSpec(memory_space=pltpu.SMEM)
    dma = pltpu.SemaphoreType.DMA
    outs = [jax.ShapeDtypeStruct((texts, width), F32)] * 2
    out_specs = [vm, vm]
    eg_shape = (total, SLOT, width)
    scratch = [
        pltpu.VMEM((SLOT, width), BF16),
        pltpu.VMEM((1024, width) if spill else (16, width), BF16),
        pltpu.VMEM((2, ff, width), BF16),
        pltpu.VMEM((ffg, width), BF16),
        pltpu.VMEM((ffg, width), BF16),
        pltpu.VMEM((2, micros, 2, rows, width), BF16),
        pltpu.VMEM((2, micros, 2, rows, width), F32),
        pltpu.VMEM((2, micros, rows, width), BF16),
        pltpu.VMEM((2, micros, rows, width), BF16),
        pltpu.VMEM((2, micros, rows, width), BF16),
        pltpu.VMEM((micros, rows, width), BF16),
        pltpu.VMEM((2 * tiles, kept, ffg), F32),
        pltpu.VMEM((imgs, ffg), F32),
        pltpu.VMEM((2 * tiles, kept, width), F32),
        pltpu.VMEM((imgs, width), F32),
        pltpu.VMEM((4, imgs, width), F32),
        pltpu.VMEM((groups, imgs, width), F32),
        pltpu.VMEM((groups, imgs, ff), F32),
        pltpu.VMEM((groups, imgs, ff), F32),
        pltpu.VMEM((groups, imgs, width), F32),
        pltpu.VMEM((groups, imgs, width), F32),
        dma((groups,)), dma((groups,)), dma((groups,)), dma((groups,)),
        dma((2, 2 * nzp)), dma((2, groups)),
        dma((3, micros)), dma((2, micros, 2)),
        dma((2, micros)), dma((2, micros)),
        dma((micros,)), dma((micros,)),
        dma((micros,)), dma((micros,)),
        dma((4,)), dma((4,)),
        dma((n_pipe * groups,)), dma((groups,)),
        dma, dma((n_pipe,)),
        dma((nz,)), dma((nz,)),
        dma, dma,
        dma((n_pipe,)), dma,
        dma, dma,
        dma((2,)),
    ]
    if spill:
        outs = outs + [jax.ShapeDtypeStruct(eg_shape, BF16)]
        out_specs = out_specs + [pl.BlockSpec(memory_space=pl.ANY)]
    else:
        scratch = scratch + [pltpu.VMEM(eg_shape, BF16)]
    result = pl.pallas_call(
        functools.partial(kernel, cfg),
        out_shape=outs,
        in_specs=[sm, sm, vm, vm, vm, vm, vm, vm, vm],
        out_specs=out_specs,
        scratch_shapes=scratch,
        compiler_params=pltpu.CompilerParams(
            collective_id=0, has_side_effects=True, vmem_limit_bytes=60 * 2**20),
    )(scale, shift, ids, tids, vis.reshape(micros, rows, width), up[0].T, down[0], cap, prior)
    return result[0], result[1]


def solution(mesh):
    placed = (
        P(None, "dp", None, None),
        P("pipe", None, "dp"),
        P("pipe", "dp", None),
        P(("pipe", "dp"), None),
        P(("pipe", "dp"), None),
        P(),
        P(),
        P(),
    )
    return jax.shard_map(
        body,
        mesh=mesh,
        in_specs=placed,
        out_specs=(P(("pipe", "dp"), None), P(("pipe", "dp"), None)),
        check_vma=False,
    )
```

```python
import functools

import jax
import jax.numpy as jnp
from jax import lax
from jax.experimental import pallas as pl
from jax.experimental.pallas import tpu as pltpu
from jax.sharding import PartitionSpec as P

F32, BF16 = jnp.float32, jnp.bfloat16
SLOT = 32
MID = 16
TILE = 256
NT = (((1,), (1,)), ((), ()))
NN = (((1,), (0,)), ((), ()))


def dot(a, b, dims):
    return lax.dot_general(a, b, dims, preferred_element_type=F32)


def layer_norm(values):
    shifted = values - jnp.mean(values, axis=-1, keepdims=True)
    variance = jnp.mean(shifted * shifted, axis=-1, keepdims=True)
    return (shifted * lax.rsqrt(variance + 1e-06)).astype(BF16)


def unit_rows(values):
    total = jnp.sum(values * values, axis=-1, keepdims=True)
    return (values * lax.rsqrt(total + 1e-06)).astype(BF16)


def kernel(
    cfg,
    scale_ref, shift_ref, ids_ref, tids_ref, x_ref, up_ref, down_ref, cap_ref, prior_ref,
    img_ref, txt_ref, *rest,
):
    n_pipe, n_dp, micros, rows, width, ff, texts, priors, spill = cfg
    if spill:
        eg, *rest = rest
    else:
        *rest, eg = rest
    (own, chunk, w_ref, ug, dg, xg, part, sc, rc, sz, rz, ma, ma2, mx, mx2, tp, tall,
     mq, rq, pq, bq, mq_s, mq_r, pq_s, pq_r,
     w_s, w_r, x_s, x_r, c_s, c_r, z_s, z_r, h_s, h_r, tp_s, tp_r, ta_s, ta_r,
     ea_s, ea_r, ez_s, ez_r, ey_s, ey_r, ex_s, ex_r, ec_s, ec_r, loc) = rest
    p, d = lax.axis_index("pipe"), lax.axis_index("dp")
    c, y, z = d % 2, (d // 2) % 2, d // 4
    zb, zp = z % 2, z // 2
    nz = n_dp // 4
    nzp = nz // 2
    groups = 2 * nzp
    last = n_pipe - 1
    oc, oz = 1 - c, 1 - zb

    def at(z_, y_, c_):
        return (z_ * 2 + y_) * 2 + c_

    d_c, d_y, d_z = at(z, y, oc), at(z, 1 - y, c), at(zp * 2 + oz, y, c)

    def copy(src, dst, s, r, pipe, dp):
        return pltpu.make_async_remote_copy(
            src_ref=src, dst_ref=dst, send_sem=s, recv_sem=r,
            device_id=(pipe, dp), device_id_type=pl.DeviceIdType.MESH)

    def arrived(dst, r):
        copy(dst, dst, loc.at[0], r, p, d_c).wait_recv()

    def left(src, s):
        copy(src, src, s, loc.at[0], p, d_c).wait_send()

    barrier = pltpu.get_barrier_semaphore()
    total = n_pipe * n_dp

    def greet(i, _):
        t = (p * n_dp + d + i) % total
        pl.semaphore_signal(barrier, inc=1, device_id=(t // n_dp, t % n_dp),
                            device_id_type=pl.DeviceIdType.MESH)
        return 0

    lax.fori_loop(1, total, greet, 0)

    own[...] = jnp.zeros_like(own)
    own[0:texts, :] = unit_rows(cap_ref[...].astype(F32))
    own[MID:MID + priors, :] = unit_rows(prior_ref[...])

    @pl.when(p == 0)
    def _():
        for m in range(micros):
            xg[zb, m, c] = x_ref[m]

    q = zp * 2 + y

    def wslot(ref, q_):
        return ref.at[pl.ds(pl.multiple_of(q_ * ff, 16), ff), :]

    shard = up_ref.shape[0]
    for k, (ref, given) in enumerate(((ug, up_ref), (dg, down_ref))):
        w_ref[k, 0:shard, :] = given[...]
        if ff > shard:
            w_ref[k, shard:ff, :] = jnp.zeros((ff - shard, width), BF16)
        ref[pl.ds(pl.multiple_of(q * ff, 16), ff), :] = w_ref[k]
    pl.semaphore_wait(barrier, total - 1)

    big = ((0, ug), (1, dg))

    def w_own_y(k, ref):
        return copy(w_ref.at[k], wslot(ref, q), w_s.at[k, 0], w_r.at[k, q], p, d_y)

    def w_own_z(k, ref, i):
        t = at(((zp + i) % nzp) * 2 + zb, y, c)
        return copy(w_ref.at[k], wslot(ref, q), w_s.at[k, i], w_r.at[k, q], p, t)

    def w_fwd(k, ref, i):
        q_ = ((zp + i) % nzp) * 2 + y
        return copy(wslot(ref, q_), wslot(ref, q_), w_s.at[k, nzp + i], w_r.at[k, q_], p, d_y)

    def x_c(m):
        return copy(xg.at[zb, m, c], xg.at[zb, m, c], x_s.at[0, m], x_r.at[zb, m, c], p, d_c)

    def x_z(m):
        return copy(xg.at[zb, m, c], xg.at[zb, m, c], x_s.at[1, m], x_r.at[zb, m, c], p, d_z)

    def x_f(m):
        return copy(xg.at[oz, m, c], xg.at[oz, m, c], x_s.at[2, m], x_r.at[oz, m, c], p, d_c)

    def w_start(k, ref):
        for i in range(1, nzp):
            w_own_z(k, ref, i).start()
        w_own_y(k, ref).start()

    def w_on(k, ref):
        for i in range(1, nzp):
            q_ = ((zp + i) % nzp) * 2 + y
            arrived(wslot(ref, q_), w_r.at[k, q_])
            w_fwd(k, ref, i).start()

    def w_here(k, ref):
        for i in range(nzp):
            q_ = ((zp + i) % nzp) * 2 + 1 - y
            arrived(wslot(ref, q_), w_r.at[k, q_])

    def eslot(index, count):
        return eg.at[pl.ds(index, count)]

    e_own = ((c * 2 + y) * nz + z) * n_pipe + p
    e_z, e_y, e_c = ((c * 2 + y) * nz + z) * n_pipe, (c * 2 + y) * nz * n_pipe, c * 2 * nz * n_pipe
    many = 2 * nz * n_pipe
    send_a = copy(own, eg.at[e_own], ea_s, ea_r.at[p], last, d)
    send_y = copy(eslot(e_y, nz * n_pipe), eslot(e_y, nz * n_pipe), ey_s, ey_r, p, d_y)
    send_c = copy(eslot(e_c, many), eslot(e_c, many), ec_s, ec_r, p, d_c)

    def send_z(i):
        return copy(eslot(e_z, n_pipe), eslot(e_z, n_pipe), ez_s.at[i], ez_r.at[z], p,
                    at((z + i) % nz, y, c))

    def send_x(i):
        return copy(eslot(e_c, many), eslot(e_c, many), ex_s.at[i], ex_r, (p + i) % n_pipe, d)

    def tokens_on():
        for m in range(micros):
            arrived(xg.at[oz, m, c], x_r.at[oz, m, c])
            x_f(m).start()

    def tokens_here():
        for m in range(micros):
            arrived(xg.at[zb, m, oc], x_r.at[zb, m, oc])
            arrived(xg.at[oz, m, oc], x_r.at[oz, m, oc])

    w_start(0, ug)

    @pl.when(p == 0)
    def _():
        for m in range(micros):
            x_c(m).start()
            x_z(m).start()

    @pl.when(p != last)
    def _():
        send_a.start()
        w_on(0, ug)
        w_start(1, dg)

    @pl.when(p == 0)
    def _():
        tokens_on()

    @pl.when(p == last)
    def _():
        keep = pltpu.make_async_copy(own, eg.at[e_own], loc.at[1])
        keep.start()
        keep.wait()
        for t in range(last):
            arrived(eg.at[e_z + t], ea_r.at[t])
        for i in range(1, nz):
            send_z(i).start()
        w_on(0, ug)
        for i in range(1, nz):
            t = (z + i) % nz
            arrived(eslot(e_y + t * n_pipe, n_pipe), ez_r.at[t])
        send_y.start()
        arrived(eslot((c * 2 + 1 - y) * nz * n_pipe, nz * n_pipe), ey_r)
        send_c.start()
        for i in range(1, n_pipe):
            send_x(i).start()
        w_here(0, ug)
        arrived(eslot(oc * many, many), ec_r)

    @pl.when(p != last)
    def _():
        w_on(1, dg)
        w_here(0, ug)

    if spill:
        ids_all, tids_all = ids_ref, tids_ref
    else:
        count = ids_ref.shape[1]
        square = (lax.broadcasted_iota(jnp.int32, (count, count), 0)
                  == lax.broadcasted_iota(jnp.int32, (count, count), 1))
        matches = jnp.max(jnp.where(square, ids_ref[...], -1), axis=1, keepdims=True)

        def look_up(index):
            shape = (count, index.shape[1])
            hit = lax.broadcasted_iota(jnp.int32, shape, 0) == index
            return jnp.max(jnp.where(hit, matches, -2), axis=0, keepdims=True)

        lane = lax.broadcasted_iota(jnp.int32, (1, total * SLOT), 1)
        s, r = lane // SLOT, lane % SLOT
        unit = s // n_pipe
        home = (s % n_pipe) * n_dp + ((unit % nz) * 2 + (unit // nz) % 2) * 2 + unit // (2 * nz)
        images = jnp.where((r >= MID) & (r < MID + priors), home * texts + 1 + r - MID, -1)
        ids_all = jnp.where(r < texts, home * texts + r, look_up(images))
        lane = lax.broadcasted_iota(jnp.int32, (1, 128), 1)
        m_, b_ = (lane // 2) % micros, (lane // (2 * micros)) % 2
        y_, z_ = (lane // (4 * micros)) % 2, lane // (8 * micros)
        home = m_ * n_dp + ((z_ * 2 + b_) * 2 + y_) * 2 + lane % 2
        tids_all = look_up(jnp.where(lane < tall.shape[0] * tall.shape[1], home * texts, -1))

    span = micros * 2 * rows
    tile = min(TILE, span)
    tiles = span // tile
    per = tile // rows
    mt = per // 2

    def activate(b, j):
        values = xg[b, pl.ds(j * mt, mt)].reshape(tile, width).astype(F32)
        act = jax.nn.gelu(dot(layer_norm(values), ug[...], NT), approximate=True)
        return values, act.astype(BF16)

    def hidden_out(m):
        return copy(sz.at[1, m], xg.at[zb, m, c], h_s.at[m], h_r.at[m],
                    jnp.minimum(p + 1, last), d)

    def to_core(b, m):
        return copy(sc.at[b, m], rc.at[b, m], c_s.at[b, m], c_r.at[b, m], p, d_c)

    def to_z(m):
        return copy(sz.at[0, m], rz.at[m], z_s.at[m], z_r.at[m], p, d_z)

    def take_hidden():
        for m in range(micros):
            arrived(xg.at[zb, m, c], h_r.at[m])
            x_c(m).start()
            x_z(m).start()
        tokens_on()

    @pl.when((p > 0) & (p < last))
    def _():
        take_hidden()

    @pl.when(p < last)
    def _():
        tokens_here()
        if tiles > 1:
            w_here(1, dg)
        for b in (oz, zb):
            def step(j, _, b=b):
                _, act = activate(b, j)
                if b is oz and tiles == 1:
                    w_here(1, dg)
                out = dot(act, dg[...], NN)
                part[b, pl.ds(j * mt, mt)] = out.reshape(mt, 2, rows, width)
                return 0

            if tiles == 1:
                step(0, 0)
            else:
                lax.fori_loop(0, tiles, step, 0)
            for m in range(micros):
                sc[b, m] = part[b, m, oc].astype(BF16)
                to_core(b, m).start()
            if b is oz:
                for m in range(micros):
                    arrived(rc.at[oz, m], c_r.at[oz, m])
                    sz[0, m] = (part[oz, m, c] + rc[oz, m].astype(F32)).astype(BF16)
                    to_z(m).start()
        for m in range(micros):
            arrived(rc.at[zb, m], c_r.at[zb, m])
            arrived(rz.at[m], z_r.at[m])
            new = part[zb, m, c] + rc[zb, m].astype(F32) + rz[m].astype(F32)
            sz[1, m] = (new + xg[zb, m, c].astype(F32)).astype(BF16)
            hidden_out(m).start()
        for m in range(micros):
            for b in range(2):
                left(sc.at[b, m], c_s.at[b, m])
            left(sz.at[0, m], z_s.at[m])
            left(sz.at[1, m], h_s.at[m])

        arrived(eslot(e_c, many), ex_r)
        send_c.start()
        arrived(eslot(oc * many, many), ec_r)

    scale, shift = scale_ref[0], shift_ref[0]
    n_rows = total * SLOT
    cs = chunk.shape[0] if spill else n_rows
    ids_w = n_rows

    def column(ref, first, count, limit):
        lane = lax.broadcasted_iota(jnp.int32, (count, limit), 1)
        row = lax.broadcasted_iota(jnp.int32, (count, limit), 0)
        return jnp.max(jnp.where(lane == row + first, ref[...], -1), axis=1, keepdims=True)

    def weigh(scores, row_ids, col_ids, keep_mask):
        logits = scale * scores + shift
        positive = row_ids == col_ids
        w = jnp.where(positive, -scale * jax.nn.sigmoid(-logits), scale * jax.nn.sigmoid(logits))
        return jnp.where(keep_mask, w, 0.0).astype(BF16)

    def block(j):
        if not spill:
            return eg[...].reshape(n_rows, width), ids_all
        fetch = pltpu.make_async_copy(eg.at[pl.ds(j * (cs // SLOT), cs // SLOT)], chunk2, loc.at[1])
        fetch.start()
        fetch.wait()
        return chunk2[...].reshape(cs, width), ids_all[:, pl.ds(pl.multiple_of(j * cs, cs), cs)]

    chunk2 = chunk.reshape(cs // SLOT, SLOT, width) if spill else None
    own_v = own[...]
    own_ids = column(ids_all, e_own * SLOT, SLOT, ids_w)
    kind_r = lax.broadcasted_iota(jnp.int32, (SLOT, cs), 0)
    kind_c = lax.broadcasted_iota(jnp.int32, (SLOT, cs), 1) % SLOT
    text_c = kind_c < texts
    prior_c = (kind_c >= MID) & (kind_c < MID + priors)
    mask = ((kind_r < texts) & prior_c) | ((kind_r >= MID) & text_c)

    def early(j, acc):
        e, ids = block(j)
        w = weigh(dot(own_v, e, NT), own_ids, ids, mask)
        return acc + dot(w, e, NN)

    if spill:
        grads = lax.fori_loop(0, n_rows // cs, early, jnp.zeros((SLOT, width), F32))
    else:
        grads = early(0, 0.0)
    img_ref[1:1 + priors, :] = grads[MID:MID + priors]

    @pl.when(p == last)
    def _():
        def step(i, _):
            b, j = i // tiles, i % tiles
            values, act = activate(b, j)
            ma[i] = jnp.mean(act.astype(F32).reshape(per, rows, -1), axis=1)
            mx[i] = jnp.mean(values.reshape(per, rows, width), axis=1)
            return 0

        take_hidden()
        tokens_here()
        lax.fori_loop(0, 2 * tiles, step, 0)
        for i in range(2 * tiles):
            ma2[i * per:(i + 1) * per, :] = ma[i]
            mx2[i * per:(i + 1) * per, :] = mx[i]
        t = zb * 2 + c
        for g in range(groups):
            mq[g] = ma2[:, g * ff:(g + 1) * ff]
        rq[q] = mq[q]

        def across(src, dst, ss, rr, i):
            g = (q + i) % groups
            return copy(src.at[g], dst.at[q], ss.at[i], rr.at[q], p,
                        at((g // 2) * 2 + zb, g % 2, c))

        for i in range(1, groups):
            across(mq, rq, mq_s, mq_r, i).start()
        for i in range(1, groups):
            g = (q + i) % groups
            arrived(rq.at[g], mq_r.at[g])
        means = rq[...].reshape(groups * rq.shape[1], ff).astype(BF16)
        pq[...] = dot(means, w_ref[1, 0:ff, :], NN).reshape(pq.shape)
        bq[q] = pq[q]
        for i in range(1, groups):
            across(pq, bq, pq_s, pq_r, i).start()
        for i in range(1, groups):
            g = (q + i) % groups
            arrived(bq.at[g], pq_r.at[g])
        tp[t] = jnp.sum(bq[...], axis=0)
        for i in range(1, groups):
            left(mq.at[q], mq_s.at[i])
            left(pq.at[q], pq_s.at[i])

        def t_out(i):
            t_ = (t + i) % 4
            return copy(tp.at[t], tp.at[t], tp_s.at[i], tp_r.at[t], p,
                        at(zp * 2 + t_ // 2, y, t_ % 2))

        for i in range(1, 4):
            t_out(i).start()
        for i in range(1, 4):
            t_ = (t + i) % 4
            arrived(tp.at[t_], tp_r.at[t_])
        pooled = mx2[...] + (tp[0] + tp[1]) + (tp[2] + tp[3])
        tall[q] = unit_rows(pooled).astype(F32)

        def spread(i, _):
            s = (last * groups + q + i) % (n_pipe * groups)
            g = s % groups
            copy(tall.at[q], tall.at[q], ta_s.at[i], ta_r.at[q], s // groups,
                 at((g // 2) * 2 + zb, g % 2, c)).start()
            return 0

        lax.fori_loop(1, n_pipe * groups, spread, 0)
        for i in range(1, 4):
            left(tp.at[t], tp_s.at[i])
        for i in range(1, groups):
            g = (q + i) % groups
            arrived(tall.at[g], ta_r.at[g])
        for i in range(1, n_pipe * groups):
            left(tall.at[q], ta_s.at[i])

    @pl.when(p != last)
    def _():
        for g in range(groups):
            arrived(tall.at[g], ta_r.at[g])

    n_t = tall.shape[0] * tall.shape[1]
    towers = tall[...].reshape(n_t, width).astype(BF16)
    t_ids = tids_all[...][:, :n_t]
    rmask = lax.broadcasted_iota(jnp.int32, (SLOT, n_t), 0) < texts
    w = weigh(dot(own_v, towers, NT), own_ids, t_ids, rmask)
    txt_ref[...] = (grads + dot(w, towers, NN))[:texts]

    mine = (zb * micros + p) * 2 + c
    pick = lax.broadcasted_iota(jnp.int32, (tall.shape[1], width), 0) == mine
    row = jnp.sum(jnp.where(pick, tall[q], 0.0), axis=0, keepdims=True)
    row8 = jnp.broadcast_to(row, (8, width)).astype(BF16)
    row_id = column(tids_all, q * tall.shape[1] + mine, 1, tids_all.shape[1])
    row_ids = jnp.broadcast_to(row_id, (8, 1))

    def late(j, acc):
        e, ids = block(j)
        w = weigh(dot(row8, e, NT), row_ids, ids, text_c[:8])
        return acc + dot(w, e, NN)

    if spill:
        g_row = lax.fori_loop(0, n_rows // cs, late, jnp.zeros((8, width), F32))
    else:
        g_row = late(0, 0.0)
    img_ref[0:1, :] = g_row[0:1]

    def gone(k):
        for i in range(nzp):
            left(w_ref.at[k], w_s.at[k, i])
        for i in range(1, nzp):
            left(w_ref.at[k], w_s.at[k, nzp + i])

    gone(0)
    pl.when(p < last)(lambda: gone(1))
    for m in range(micros):
        for i in range(3):
            left(xg.at[zb, m, c], x_s.at[i, m])
    send_c.wait_send()

    @pl.when(p == last)
    def _():
        for i in range(1, nz):
            left(eslot(e_z, n_pipe), ez_s.at[i])
        send_y.wait_send()
        for i in range(1, n_pipe):
            left(eslot(e_c, many), ex_s.at[i])

    @pl.when(p != last)
    def _():
        send_a.wait_send()


def id_rows(match, n_pipe, nz, texts, priors):
    total = n_pipe * nz * 4

    def placed(numbers):
        numbers = numbers.reshape(n_pipe, nz, 2, 2, texts)
        return numbers.transpose(3, 2, 1, 0, 4).reshape(total, texts)

    ids = jnp.concatenate([
        jnp.pad(placed(jnp.arange(total * texts, dtype=jnp.int32)),
                ((0, 0), (0, MID - texts)), constant_values=-2),
        jnp.pad(placed(match)[:, 1:], ((0, 0), (0, SLOT - MID - priors)), constant_values=-2),
    ], axis=1).reshape(1, total * SLOT)
    tids = match.reshape(n_pipe, nz // 2, 2, 2, 2, texts)[..., 0]
    tids = tids.transpose(1, 3, 2, 0, 4).reshape(1, -1)
    tids = jnp.pad(tids, ((0, 0), (0, -tids.shape[1] % 128)), constant_values=-2)
    return ids, tids


def body(vis, up, down, cap, prior, match, scale, shift):
    n_pipe, n_dp = lax.axis_size("pipe"), lax.axis_size("dp")
    micros, img_mb, patch, width = vis.shape
    rows = img_mb * patch
    shard = up.shape[2]
    ff = -(-shard // 16) * 16
    texts, priors = cap.shape[0], prior.shape[0]
    nz, total = n_dp // 4, n_pipe * n_dp
    nzp = nz // 2
    groups = 2 * nzp
    spill = total > 64
    if spill:
        ids, tids = id_rows(match, n_pipe, nz, texts, priors)
    else:
        ids = tids = match.reshape(1, -1)
    cfg = (n_pipe, n_dp, micros, rows, width, ff, texts, priors, spill)
    span = micros * 2 * rows
    tile = min(TILE, span)
    tiles, kept = span // tile, tile // rows
    imgs = 4 * micros
    ffg = groups * ff
    vm = pl.BlockSpec(memory_space=pltpu.VMEM)
    sm = pl.BlockSpec(memory_space=pltpu.SMEM)
    dma = pltpu.SemaphoreType.DMA
    outs = [jax.ShapeDtypeStruct((texts, width), F32)] * 2
    out_specs = [vm, vm]
    eg_shape = (total, SLOT, width)
    scratch = [
        pltpu.VMEM((SLOT, width), BF16),
        pltpu.VMEM((1024, width) if spill else (16, width), BF16),
        pltpu.VMEM((2, ff, width), BF16),
        pltpu.VMEM((ffg, width), BF16),
        pltpu.VMEM((ffg, width), BF16),
        pltpu.VMEM((2, micros, 2, rows, width), BF16),
        pltpu.VMEM((2, micros, 2, rows, width), F32),
        pltpu.VMEM((2, micros, rows, width), BF16),
        pltpu.VMEM((2, micros, rows, width), BF16),
        pltpu.VMEM((2, micros, rows, width), BF16),
        pltpu.VMEM((micros, rows, width), BF16),
        pltpu.VMEM((2 * tiles, kept, ffg), F32),
        pltpu.VMEM((imgs, ffg), F32),
        pltpu.VMEM((2 * tiles, kept, width), F32),
        pltpu.VMEM((imgs, width), F32),
        pltpu.VMEM((4, imgs, width), F32),
        pltpu.VMEM((groups, imgs, width), F32),
        pltpu.VMEM((groups, imgs, ff), F32),
        pltpu.VMEM((groups, imgs, ff), F32),
        pltpu.VMEM((groups, imgs, width), F32),
        pltpu.VMEM((groups, imgs, width), F32),
        dma((groups,)), dma((groups,)), dma((groups,)), dma((groups,)),
        dma((2, 2 * nzp)), dma((2, groups)),
        dma((3, micros)), dma((2, micros, 2)),
        dma((2, micros)), dma((2, micros)),
        dma((micros,)), dma((micros,)),
        dma((micros,)), dma((micros,)),
        dma((4,)), dma((4,)),
        dma((n_pipe * groups,)), dma((groups,)),
        dma, dma((n_pipe,)),
        dma((nz,)), dma((nz,)),
        dma, dma,
        dma((n_pipe,)), dma,
        dma, dma,
        dma((2,)),
    ]
    if spill:
        outs = outs + [jax.ShapeDtypeStruct(eg_shape, BF16)]
        out_specs = out_specs + [pl.BlockSpec(memory_space=pl.ANY)]
    else:
        scratch = scratch + [pltpu.VMEM(eg_shape, BF16)]
    result = pl.pallas_call(
        functools.partial(kernel, cfg),
        out_shape=outs,
        in_specs=[sm, sm, vm, vm, vm, vm, vm, vm, vm],
        out_specs=out_specs,
        scratch_shapes=scratch,
        compiler_params=pltpu.CompilerParams(
            collective_id=0, has_side_effects=True, vmem_limit_bytes=60 * 2**20),
    )(scale, shift, ids, tids, vis.reshape(micros, rows, width), up[0].T, down[0], cap, prior)
    return result[0], result[1]


def solution(mesh):
    placed = (
        P(None, "dp", None, None),
        P("pipe", None, "dp"),
        P("pipe", "dp", None),
        P(("pipe", "dp"), None),
        P(("pipe", "dp"), None),
        P(),
        P(),
        P(),
    )
    return jax.shard_map(
        body,
        mesh=mesh,
        in_specs=placed,
        out_specs=(P(("pipe", "dp"), None), P(("pipe", "dp"), None)),
        check_vma=False,
    )
```
